256 devices in a mesh: rows: 4 (over y_lo, core), shard: 64 (over x, y_hi, z).
Axes of the slice: x: 4, y: 4 (y_hi: 2, y_lo: 2; y = y_hi * 2 + y_lo), z: 8, core: 2. Of those that a mesh axis runs over, the one named last changes fastest.
Arguments:
- hidden_in: bfloat16 [128, 14336], P('rows', 'shard'), may hold values from -6 to 6
- resid: bfloat16 [128, 3584], P('rows'), may hold values from -6 to 6
- down_one: bfloat16 [14336, 3584], P('shard'), may hold values from -0.046875 to 0.046875
- gain_one: float32 [3584], replicated, may hold values from 0.5 to 1.5
- enc_weight: bfloat16 [3584, 65536], P(None, ('rows', 'shard')), may hold values from -0.09375 to 0.09375
- enc_bias: float32 [65536], P(('rows', 'shard')), may hold values from -3 to 3
- dec_weight: bfloat16 [65536, 3584], P(('rows', 'shard')), may hold values from -0.09375 to 0.09375
- dec_bias: float32 [3584], replicated, may hold values from -3 to 3
- gain_pre: float32 [3584], replicated, may hold values from 0.5 to 1.5
- gate_two: bfloat16 [3584, 14336], P(None, 'shard'), may hold values from -0.09375 to 0.09375
- up_two: bfloat16 [3584, 14336], P(None, 'shard'), may hold values from -0.09375 to 0.09375
- down_two: bfloat16 [14336, 3584], P('shard'), may hold values from -0.046875 to 0.046875
- gain_post: float32 [3584], replicated, may hold values from 0.5 to 1.5
Outputs:
- latents: bfloat16 [128, 65536], P(None, ('rows', 'shard'))
- delta: float32 [128, 3584], P('rows', 'shard')
The draws below stay inside these ranges and needn't reach their ends.
All inputs are finite; a program needn't handle non-finite values.
Results may differ from the reference program's by a relative error of at most 0.0064.
Values may be sent and summed in bfloat16 or wider, within the bound.
A program may use at most 64 MiB of HBM per device.

```python
import jax
import jax.numpy as jnp
from jax import lax

D = 3584
FF = 14336
LAT = 65536
TOKENS = 128


def raised(result, own_key, source, target, blocks, factor):
    owner, partner = [(jnp.arange(result.shape[dim]) // (result.shape[dim] // blocks)).reshape([-1 if axis == dim else 1 for axis in range(result.ndim)]) for dim in (source, target)]
    chosen = jax.random.permutation(own_key, blocks)[partner]
    strong = (owner == chosen) | (owner == (partner + blocks // 2) % blocks)
    return jnp.where(strong, factor * result, result)


def levels(own_key, extent, pieces, least, high):
    factor_of, own = 1.0, jax.random.fold_in(own_key, 6)
    for axis_at, parts in pieces:
        heights = jnp.exp(jax.random.uniform(jax.random.fold_in(own, axis_at), (parts,), jnp.float32, least / len(pieces), high / len(pieces)))
        factor_of = factor_of * jnp.repeat(heights, extent[axis_at] // parts).reshape([-1 if axis == axis_at else 1 for axis in range(len(extent))])
    return factor_of


def bell_draw(rng, extent, scale, limit, cuts=(), held_as=jnp.bfloat16):
    level = levels(rng, extent, cuts, -0.22, 0.18) if cuts else 1.0
    values = jax.random.normal(rng, extent, jnp.float32) * scale * level
    return jnp.minimum(jnp.maximum(values, -limit), limit).astype(held_as)


def gaussian_with(own_key, shape, width, limit, cuts, heavy, kind=jnp.bfloat16):
    drawn = width * jax.random.normal(own_key, shape, jnp.float32)
    if cuts:
        drawn = drawn * levels(own_key, shape, cuts, -0.22, 0.18)
    return jnp.clip(raised(drawn, jax.random.fold_in(own_key, 3), *heavy), -limit, limit).astype(kind)


def setup_inputs(seed: int = 0) -> dict:
    keys = jax.random.split(jax.random.key(seed), 14)
    hidden_in = bell_draw(keys[0], (TOKENS, FF), 1.0, 6.0, ((0, 4), (1, 64)))
    resid = bell_draw(keys[1], (TOKENS, D), 1.0, 6.0, ((0, 4),))
    down_one = bell_draw(keys[2], (FF, D), FF ** -0.5, 0.046875, ((0, 64),))
    gain_one = jnp.clip(jax.random.uniform(keys[3], (D,), jnp.float32, 0.5, 1.5), 0.5, 1.5)
    enc_weight = bell_draw(keys[4], (D, LAT), D ** -0.5, 0.09375, ((1, 256),))
    enc_bias = bell_draw(keys[5], (LAT,), 0.5, 3.0, ((0, 256),), jnp.float32)
    dec_weight = gaussian_with(keys[6], (LAT, D), LAT ** -0.5, 0.09375, ((0, 256),), (0, 1, 256, 6.0))
    dec_bias = bell_draw(keys[7], (D,), 0.5, 3.0, (), jnp.float32)
    gain_pre = jnp.clip(jax.random.uniform(keys[8], (D,), jnp.float32, 0.5, 1.5), 0.5, 1.5)
    gate_two = bell_draw(keys[9], (D, FF), D ** -0.5, 0.09375, ((1, 64),))
    up_two = bell_draw(keys[10], (D, FF), D ** -0.5, 0.09375, ((1, 64),))
    down_two = bell_draw(keys[11], (FF, D), FF ** -0.5, 0.046875, ((0, 64),))
    gain_post = jnp.clip(jax.random.uniform(keys[12], (D,), jnp.float32, 0.5, 1.5), 0.5, 1.5)
    return dict(hidden_in=hidden_in, resid=resid, down_one=down_one, gain_one=gain_one, enc_weight=enc_weight, enc_bias=enc_bias, dec_weight=dec_weight, dec_bias=dec_bias, gain_pre=gain_pre, gate_two=gate_two, up_two=up_two, down_two=down_two, gain_post=gain_post)


def rms_scale(values, gain):
    mean_sq = lax.optimization_barrier(jnp.mean(values * values, axis=1, keepdims=True))
    return values * jax.lax.rsqrt(mean_sq + 1e-06) * gain

def layer_two(stream, gain_pre, gate_two, up_two, down_two, gain_post):
    upcast = stream.astype(jnp.float32)
    normed = rms_scale(upcast, gain_pre).astype(jnp.bfloat16)
    gate_out = jnp.dot(normed, gate_two, preferred_element_type=jnp.float32)
    up_out = jnp.dot(normed, up_two, preferred_element_type=jnp.float32)
    act = (jax.nn.gelu(gate_out, approximate=True) * up_out).astype(jnp.bfloat16)
    second = jnp.dot(act, down_two, preferred_element_type=jnp.float32)
    return upcast + rms_scale(second, gain_post)

def reference(hidden_in, resid, down_one, gain_one, enc_weight, enc_bias, dec_weight, dec_bias, gain_pre, gate_two, up_two, down_two, gain_post):
    first = jnp.dot(hidden_in, down_one, preferred_element_type=jnp.float32)
    clean = (resid.astype(jnp.float32) + rms_scale(first, gain_one)).astype(jnp.bfloat16)
    centered = (clean.astype(jnp.float32) - dec_bias).astype(jnp.bfloat16)
    pre_act = jnp.dot(centered, enc_weight, preferred_element_type=jnp.float32) + enc_bias
    latents = jnp.maximum(pre_act, 0.0).astype(jnp.bfloat16)
    recon = (jnp.dot(latents, dec_weight, preferred_element_type=jnp.float32) + dec_bias).astype(jnp.bfloat16)
    out_clean = layer_two(clean, gain_pre, gate_two, up_two, down_two, gain_post)
    out_recon = layer_two(recon, gain_pre, gate_two, up_two, down_two, gain_post)
    return (latents, out_recon - out_clean)
```

```python
import functools

import jax
import jax.numpy as jnp
from jax import lax
from jax.experimental import pallas as pl
from jax.experimental.pallas import tpu as pltpu
from jax.sharding import PartitionSpec as P

D = 3584
T = D // 128
MESH = pl.DeviceIdType.MESH
F32, BF16 = jnp.float32, jnp.bfloat16
EPS = 1e-06


def pick(ref, start, rows):
    tile, turn = start // 128, lax.rem(start, 128)
    lo = ref[0:rows, pl.ds(pl.multiple_of(tile * 128, 128), 128)]
    hi = ref[0:rows, pl.ds(pl.multiple_of(tile * 128 + 128, 128), 128)]
    shift = lax.rem(128 - turn, 128)
    lane = lax.broadcasted_iota(jnp.int32, (rows, 128), 1)
    return jnp.where(lane < 128 - turn, pltpu.roll(lo, shift, 1), pltpu.roll(hi, shift, 1))


def gelu(v):
    return 0.5 * v * (1.0 + jnp.tanh(0.7978845608028654 * (v + 0.044715 * (v * v * v))))


def kernel(
    hid_h, resid_h, d1_h, g1_h, enc_h, eb_h, dec_h, db_h, gpre_h, gate_h, up_h, d2_h, gpost_h,
    lat_o, delta_o,
    hid, resid, d1, g1, enc, eb, dec, db, gpre, gate, up, d2, gpost,
    parts, parts_b, land_b1, send_b2, land_b2, resid_c, g1_c, db_c, db_row, gpre_row, gpost_row,
    clean_all, cent, lhs, lat, pre_src, pre_land, e_src, e_own, land_e1, send_e2, land_e2, recon_p,
    clean_u, recon_u, lhs_f, f_src, f_own, land_f1, f_sum, send_f2, land_f2, second, send_f3, land_f3,
    load_sem, s_b1, r_b1, s_b2, r_b2, s_c, r_c, s_cc, r_cc, s_p, r_p, s_e1, r_e1, s_e2, r_e2, s_e3, r_e3,
    s_f1, r_f1, s_f2, r_f2, s_f3, r_f3,
):
    r = lax.axis_index("rows")
    s = lax.axis_index("shard")
    yl, c = r // 2, lax.rem(r, 2)
    k, z = s // 8, lax.rem(s, 8)
    x, yh = k // 2, lax.rem(k, 2)
    m = yl * 8 + k
    other = (yl * 2 + 1 - c, s)

    def in_k(i):
        return (r, lax.rem(k + i, 8) * 8 + z)

    def in_z(i):
        return (r, k * 8 + lax.rem(z + i, 8))

    def in_plane(i):
        to = lax.rem(m + i, 16)
        return ((to // 8) * 2 + c, lax.rem(to, 8) * 8 + z)

    def send(src, dst, s_sem, r_sem, device):
        return pltpu.make_async_remote_copy(
            src_ref=src, dst_ref=dst, send_sem=s_sem, recv_sem=r_sem, device_id=device, device_id_type=MESH
        )

    loads = [
        pltpu.make_async_copy(a, b, load_sem.at[i])
        for i, (a, b) in enumerate(
            (
                (hid_h, hid), (d1_h, d1), (resid_h, resid), (g1_h, g1), (db_h, db), (gpre_h, gpre), (gpost_h, gpost),
                (eb_h, eb), (enc_h, enc), (dec_h, dec), (gate_h, gate), (up_h, up), (d2_h, d2),
            )
        )
    ]
    for load in loads:
        load.start()

    barrier = pltpu.get_barrier_semaphore()

    @pl.loop(1, 16)
    def _(i):
        pl.semaphore_signal(barrier, inc=1, device_id=in_plane(i), device_id_type=MESH)

    @pl.loop(1, 8)
    def _(i):
        pl.semaphore_signal(barrier, inc=1, device_id=in_z(i), device_id_type=MESH)

    pl.semaphore_signal(barrier, inc=1, device_id=other, device_id_type=MESH)

    loads[0].wait()
    loads[1].wait()
    for g in range(7):
        part = jnp.dot(hid[...], d1[:, 512 * g : 512 * g + 512], preferred_element_type=F32)
        for j in range(4):
            row = 4 * (4 * g + j)
            for piece in range(8):
                parts[piece, row : row + 4, :] = part[4 * piece : 4 * piece + 4, 128 * j : 128 * j + 128]
    for piece in range(8):
        parts_b[piece] = parts[piece].astype(BF16)

    pl.semaphore_wait(barrier, 23)

    def b1(i):
        return send(parts_b.at[lax.rem(k + i, 8)], land_b1.at[i], s_b1.at[i], r_b1.at[i], in_k(i))

    @pl.loop(1, 8)
    def _(i):
        b1(i).start()

    for i in range(2, 8):
        loads[i].wait()
    for j in range(T):
        tile = slice(128 * j, 128 * j + 128)
        old = resid[:, tile].astype(F32)
        for piece in range(8):
            resid_c[piece, 4 * j : 4 * j + 4, :] = old[4 * piece : 4 * piece + 4, :]
        g1_c[4 * j : 4 * j + 4, :] = jnp.broadcast_to(g1[j : j + 1, :], (4, 128))
        db_c[4 * j : 4 * j + 4, :] = jnp.broadcast_to(db[j : j + 1, :], (4, 128))
        gpre_row[:, tile] = jnp.broadcast_to(gpre[j : j + 1, :], (8, 128))
        gpost_row[:, tile] = jnp.broadcast_to(gpost[j : j + 1, :], (8, 128))
        db_row[j // 7, :, 128 * (j % 7) : 128 * (j % 7) + 128] = jnp.broadcast_to(db[j : j + 1, :], (8, 128))
    gpost_row[:, D:] = jnp.zeros((8, 128), F32)
    clean_u[:, D:] = jnp.zeros((32, 128), F32)
    recon_u[:, D:] = jnp.zeros((32, 128), F32)
    second[:, :, 448:] = jnp.zeros((2, 32, 192), F32)
    f_src[:, :, :, 448:] = jnp.zeros((2, 8, 32, 64), BF16)
    f_own[:, :, :, 448:] = jnp.zeros((2, 8, 32, 64), F32)

    for i in range(1, 8):
        b1(i).wait_recv()
    total = parts[k]
    for i in range(1, 8):
        total += land_b1[i].astype(F32)
    send_b2[...] = total.astype(BF16)

    def b2(i):
        return send(send_b2, land_b2.at[i], s_b2.at[i], r_b2.at[i], in_z(i))

    @pl.loop(1, 8)
    def _(i):
        b2(i).start()

    for i in range(1, 8):
        b2(i).wait_recv()
    for i in range(1, 8):
        total += land_b2[i].astype(F32)
    squares = total[0:8] * total[0:8]
    for i in range(1, 14):
        squares += total[8 * i : 8 * i + 8] * total[8 * i : 8 * i + 8]
    squares += pltpu.roll(squares, 4, 0)
    scale = lax.rsqrt(jnp.sum(squares, axis=1, keepdims=True) / D + EPS)
    scale = jnp.concatenate([jnp.broadcast_to(scale, (8, 128))] * 14, axis=0)
    mine = r * 8 + k
    clean_all[mine] = (resid_c[k] + total * scale * g1_c[...]).astype(BF16)

    def spread(i):
        return send(clean_all.at[mine], clean_all.at[mine], s_c.at[i], r_c.at[i], in_plane(i))

    def arrival(i):
        source = lax.rem(m + 16 - i, 16)
        at = ((source // 8) * 2 + c) * 8 + lax.rem(source, 8)
        return send(clean_all.at[at], clean_all.at[at], s_c.at[i], r_c.at[i], in_plane(i)), at

    def forward(i, at):
        return send(clean_all.at[at], clean_all.at[at], s_cc.at[i], r_cc.at[i], other)

    @pl.loop(1, 16)
    def _(i):
        spread(i).start()

    forward(0, mine).start()

    @pl.loop(1, 16)
    def _(i):
        copy, at = arrival(i)
        copy.wait_recv()
        forward(i, at).start()

    @pl.loop(0, 16)
    def _(i):
        source = lax.rem(m + 16 - i, 16)
        at = ((source // 8) * 2 + 1 - c) * 8 + lax.rem(source, 8)
        forward(i, at).wait_recv()

    for q in range(32):
        centered = (clean_all[q].astype(F32) - db_c[...]).astype(BF16).astype(F32)
        for j in range(T):
            cent[4 * q : 4 * q + 4, 128 * j : 128 * j + 128] = centered[4 * j : 4 * j + 4, :]
    lhs[...] = cent[...].astype(BF16)
    loads[8].wait()
    pre_act = jnp.dot(lhs[...], enc[...], preferred_element_type=F32) + eb[...]
    lat[...] = jnp.maximum(pre_act, 0.0).astype(BF16)
    lat_o[...] = lat[...]

    def tokens_of(core):
        low = lat[pl.ds(pl.multiple_of(core * 32, 32), 32), :]
        high = lat[pl.ds(pl.multiple_of(core * 32 + 64, 32), 32), :]
        return jnp.concatenate([low, high], axis=0)

    def to_other(g):
        return send(pre_src.at[g], pre_land.at[g], s_p.at[g], r_p.at[g], other)

    loads[9].wait()
    theirs = tokens_of(1 - c)
    for g in range(4):
        cols = slice(896 * g, 896 * g + 896)
        pre_src[g] = jnp.dot(theirs, dec[:, cols], preferred_element_type=F32).astype(BF16)
        to_other(g).start()
    ours = tokens_of(c)

    def e1(g, to_yl, to_yh):
        to = to_yl * 8 + g * 2 + to_yh
        i = lax.rem(to + 16 - m, 16)
        row = 32 * to_yl + 16 * to_yh
        return to, send(e_src.at[g, row : row + 16, :], land_e1.at[i], s_e1.at[i], r_e1.at[i], in_plane(i))

    for g in range(4):
        cols = slice(896 * g, 896 * g + 896)
        e_own[g] = jnp.dot(ours, dec[:, cols], preferred_element_type=F32)
        to_other(g).wait_recv()
        e_own[g] += pre_land[g].astype(F32)
        e_src[g] = e_own[g].astype(BF16)
        for to_yl in range(2):
            for to_yh in range(2):
                to, copy = e1(g, to_yl, to_yh)

                @pl.when(to != m)
                def _(copy=copy):
                    copy.start()

    def layer(h, stream):
        squares = jnp.zeros((32, 128), F32)
        for j in range(T):
            tile = stream[:, 128 * j : 128 * j + 128]
            squares += tile * tile
        scale = lax.rsqrt(jnp.sum(squares, axis=1, keepdims=True) / D + EPS)
        for g in range(7):
            cols = slice(512 * g, 512 * g + 512)
            lhs_f[h, :, cols] = (stream[:, cols] * scale * gpre_row[0:1, cols]).astype(BF16)
        gate_out = jnp.dot(lhs_f[h], gate[...], preferred_element_type=F32)
        up_out = jnp.dot(lhs_f[h], up[...], preferred_element_type=F32)
        act = (gelu(gate_out) * up_out).astype(BF16)
        for g in range(4):
            part = jnp.dot(act, d2[:, 896 * g : 896 * g + 896], preferred_element_type=F32)
            for half in range(2):
                piece = part[:, 448 * half : 448 * half + 448]
                f_own[h, 2 * g + half, :, 0:448] = piece
                f_src[h, 2 * g + half, :, 0:448] = piece.astype(BF16)

    for q in range(8):
        clean = clean_all[r * 8 + q].astype(F32)
        for j in range(T):
            clean_u[4 * q : 4 * q + 4, 128 * j : 128 * j + 128] = clean[4 * j : 4 * j + 4, :]
    loads[10].wait()
    loads[11].wait()
    loads[12].wait()
    layer(0, clean_u)

    for i in range(1, 16):
        send(land_e1.at[i], land_e1.at[i], s_e1.at[i], r_e1.at[i], in_plane(i)).wait_recv()
    row = pl.multiple_of(32 * yl + 16 * yh, 16)
    total = e_own[x, pl.ds(row, 16), :]
    for i in range(1, 16):
        total += land_e1[i].astype(F32)
    send_e2[...] = total.astype(BF16)

    def e2(i):
        return send(send_e2, land_e2.at[i], s_e2.at[i], r_e2.at[i], in_z(i))

    @pl.loop(1, 8)
    def _(i):
        e2(i).start()

    def f1(h, i):
        return send(f_src.at[h, lax.rem(k + i, 8)], land_f1.at[h, i], s_f1.at[h, i], r_f1.at[h, i], in_k(i))

    def f2(h, i):
        return send(send_f2.at[h], land_f2.at[h, i], s_f2.at[h, i], r_f2.at[h, i], in_z(i))

    def f3(h, i):
        return send(send_f3.at[h], land_f3.at[h, i], s_f3.at[h, i], r_f3.at[h, i], in_k(i))

    @pl.loop(1, 8)
    def _(i):
        f1(0, i).start()

    for i in range(1, 8):
        e2(i).wait_recv()
    for i in range(1, 8):
        total += land_e2[i].astype(F32)
    recon_p[k] = (total + db_row[x, 0:1, :]).astype(BF16)

    def e3(i):
        return send(recon_p.at[k], recon_p.at[k], s_e3.at[i], r_e3.at[i], in_k(i))

    @pl.loop(1, 8)
    def _(i):
        e3(i).start()

    def sum_over_k(h):
        for i in range(1, 8):
            f1(h, i).wait_recv()
        total = f_own[h, k]
        for i in range(1, 8):
            total += land_f1[h, i].astype(F32)
        f_sum[h] = total
        send_f2[h] = total.astype(BF16)

        @pl.loop(1, 8)
        def _(i):
            f2(h, i).start()

    diagonal = (
        lax.broadcasted_iota(jnp.int32, (32, 128), 0) == lax.broadcasted_iota(jnp.int32, (32, 128), 1)
    ).astype(F32)

    def sum_over_z(h):
        for i in range(1, 8):
            f2(h, i).wait_recv()
        total = f_sum[h]
        for i in range(1, 8):
            total += land_f2[h, i].astype(F32)
        second[h, :, 0:512] = total
        squares = jnp.sum(total * total, axis=1, keepdims=True)
        flat = jnp.sum(squares * diagonal, axis=0, keepdims=True)
        send_f3[h] = jnp.broadcast_to(flat, (8, 128))

        @pl.loop(1, 8)
        def _(i):
            f3(h, i).start()

    def outputs(h, stream):
        for i in range(1, 8):
            f3(h, i).wait_recv()
        flat = send_f3[h]
        for i in range(1, 8):
            flat += land_f3[h, i]
        squares = jnp.sum(flat[0:1, :] * diagonal, axis=1, keepdims=True)
        gain = pick(gpost_row, 56 * s, 8)[0:1, :]
        return pick(stream, 56 * s, 32) + pick(second.at[h], 56 * z, 32) * lax.rsqrt(squares / D + EPS) * gain

    sum_over_k(0)

    def arrived(i):
        at = lax.rem(k + 8 - i, 8)
        return send(recon_p.at[at], recon_p.at[at], s_e3.at[i], r_e3.at[i], in_k(i))

    for i in range(1, 8):
        arrived(i).wait_recv()
    for q in range(8):
        row, col = 16 * (q % 2), 896 * (q // 2)
        recon_u[row : row + 16, col : col + 896] = recon_p[q].astype(F32)
    layer(1, recon_u)

    @pl.loop(1, 8)
    def _(i):
        f1(1, i).start()

    sum_over_z(0)
    sum_over_k(1)
    clean_out = outputs(0, clean_u)
    sum_over_z(1)
    delta_o[...] = outputs(1, recon_u) - clean_out

    @pl.loop(1, 8)
    def _(i):
        b1(i).wait_send()
        b2(i).wait_send()
        e2(i).wait_send()
        e3(i).wait_send()
        for h in range(2):
            f1(h, i).wait_send()
            f2(h, i).wait_send()
            f3(h, i).wait_send()

    @pl.loop(1, 16)
    def _(i):
        spread(i).wait_send()
        send(land_e1.at[i], land_e1.at[i], s_e1.at[i], r_e1.at[i], in_plane(i)).wait_send()

    @pl.loop(0, 16)
    def _(i):
        forward(i, mine).wait_send()

    for g in range(4):
        to_other(g).wait_send()


def on_device(
    hidden_in, resid, down_one, gain_one, enc_weight, enc_bias, dec_weight, dec_bias, gain_pre, gate_two, up_two,
    down_two, gain_post,
):
    tiles = (T, 128)
    args = (
        hidden_in, resid, down_one, gain_one.reshape(tiles), enc_weight, enc_bias.reshape(1, 256), dec_weight,
        dec_bias.reshape(tiles), gain_pre.reshape(tiles), gate_two, up_two, down_two, gain_post.reshape(tiles),
    )
    dma = pltpu.SemaphoreType.DMA
    vmem = pltpu.VMEM
    latents, delta = pl.pallas_call(
        kernel,
        name="spliced",
        out_shape=(jax.ShapeDtypeStruct((128, 256), BF16), jax.ShapeDtypeStruct((32, 128), F32)),
        in_specs=[pl.BlockSpec(memory_space=pl.ANY)] * len(args),
        out_specs=[pl.BlockSpec(memory_space=pltpu.VMEM)] * 2,
        scratch_shapes=[vmem(a.shape, a.dtype) for a in args]
        + [
            vmem((8, 112, 128), F32),
            vmem((8, 112, 128), BF16),
            vmem((8, 112, 128), BF16),
            vmem((112, 128), BF16),
            vmem((8, 112, 128), BF16),
            vmem((8, 112, 128), F32),
            vmem((112, 128), F32),
            vmem((112, 128), F32),
            vmem((4, 8, 896), F32),
            vmem((8, D), F32),
            vmem((8, D + 128), F32),
            vmem((32, 112, 128), BF16),
            vmem((128, D), F32),
            vmem((128, D), BF16),
            vmem((128, 256), BF16),
            vmem((4, 64, 896), BF16),
            vmem((4, 64, 896), BF16),
            vmem((4, 64, 896), BF16),
            vmem((4, 64, 896), F32),
            vmem((16, 16, 896), BF16),
            vmem((16, 896), BF16),
            vmem((8, 16, 896), BF16),
            vmem((8, 16, 896), BF16),
            vmem((32, D + 128), F32),
            vmem((32, D + 128), F32),
            vmem((2, 32, D), BF16),
            vmem((2, 8, 32, 512), BF16),
            vmem((2, 8, 32, 512), F32),
            vmem((2, 8, 32, 512), BF16),
            vmem((2, 32, 512), F32),
            vmem((2, 32, 512), BF16),
            vmem((2, 8, 32, 512), BF16),
            vmem((2, 32, 640), F32),
            vmem((2, 8, 128), F32),
            vmem((2, 8, 8, 128), F32),
            dma((13,)),
            dma((8,)), dma((8,)), dma((8,)), dma((8,)),
            dma((16,)), dma((16,)), dma((16,)), dma((16,)),
            dma((4,)), dma((4,)), dma((16,)), dma((16,)),
            dma((8,)), dma((8,)), dma((8,)), dma((8,)),
            dma((2, 8)), dma((2, 8)), dma((2, 8)), dma((2, 8)), dma((2, 8)), dma((2, 8)),
        ],
        compiler_params=pltpu.CompilerParams(
            collective_id=0, has_side_effects=True, vmem_limit_bytes=48 * 2**20
        ),
        cost_estimate=pl.CostEstimate(flops=10**9, bytes_accessed=12 * 10**6, transcendentals=10**5),
    )(*args)
    return latents, delta[:, :56]


def solution(mesh):
    in_specs = (
        P("rows", "shard"),
        P("rows", None),
        P("shard", None),
        P(),
        P(None, ("rows", "shard")),
        P(("rows", "shard")),
        P(("rows", "shard"), None),
        P(),
        P(),
        P(None, "shard"),
        P(None, "shard"),
        P("shard", None),
        P(),
    )
    out_specs = (P(None, ("rows", "shard")), P("rows", "shard"))
    return jax.shard_map(on_device, mesh=mesh, in_specs=in_specs, out_specs=out_specs, check_vma=False)
```

```python
import functools

import jax
import jax.numpy as jnp
from jax import lax
from jax.experimental import pallas as pl
from jax.experimental.pallas import tpu as pltpu
from jax.sharding import PartitionSpec as P

D = 3584
T = D // 128
MESH = pl.DeviceIdType.MESH
F32, BF16 = jnp.float32, jnp.bfloat16
EPS = 1e-06


def pick(ref, start, rows):
    tile, turn = start // 128, lax.rem(start, 128)
    lo = ref[0:rows, pl.ds(pl.multiple_of(tile * 128, 128), 128)]
    hi = ref[0:rows, pl.ds(pl.multiple_of(tile * 128 + 128, 128), 128)]
    shift = lax.rem(128 - turn, 128)
    lane = lax.broadcasted_iota(jnp.int32, (rows, 128), 1)
    return jnp.where(lane < 128 - turn, pltpu.roll(lo, shift, 1), pltpu.roll(hi, shift, 1))


def gelu(v):
    return 0.5 * v * (1.0 + jnp.tanh(0.7978845608028654 * (v + 0.044715 * (v * v * v))))


def kernel(
    hid_h, resid_h, d1_h, g1_h, enc_h, eb_h, dec_h, db_h, gpre_h, gate_h, up_h, d2_h, gpost_h,
    lat_o, delta_o,
    hid, resid, d1, g1, enc, eb, dec, db, gpre, gate, up, d2, gpost,
    parts, parts_b, land_b1, send_b2, land_b2, resid_c, g1_c, db_c, db_row, gpre_row, gpost_row,
    clean_all, cent, lhs, lat, pre_src, pre_land, e_src, e_own, land_e1, send_e2, land_e2, recon_p,
    clean_u, recon_u, lhs_f, f_src, f_own, land_f1, f_sum, send_f2, land_f2, second, send_f3, land_f3,
    load_sem, s_b1, r_b1, s_b2, r_b2, s_c, r_c, s_cc, r_cc, s_p, r_p, s_e1, r_e1, s_e2, r_e2, s_e3, r_e3,
    s_f1, r_f1, s_f2, r_f2, s_f3, r_f3,
):
    r = lax.axis_index("rows")
    s = lax.axis_index("shard")
    yl, c = r // 2, lax.rem(r, 2)
    k, z = s // 8, lax.rem(s, 8)
    x, yh = k // 2, lax.rem(k, 2)
    m = yl * 8 + k
    other = (yl * 2 + 1 - c, s)

    def in_k(i):
        return (r, lax.rem(k + i, 8) * 8 + z)

    def in_z(i):
        return (r, k * 8 + lax.rem(z + i, 8))

    def in_plane(i):
        to = lax.rem(m + i, 16)
        return ((to // 8) * 2 + c, lax.rem(to, 8) * 8 + z)

    def send(src, dst, s_sem, r_sem, device):
        return pltpu.make_async_remote_copy(
            src_ref=src, dst_ref=dst, send_sem=s_sem, recv_sem=r_sem, device_id=device, device_id_type=MESH
        )

    loads = [
        pltpu.make_async_copy(a, b, load_sem.at[i])
        for i, (a, b) in enumerate(
            (
                (hid_h, hid), (d1_h, d1), (resid_h, resid), (g1_h, g1), (db_h, db), (gpre_h, gpre), (gpost_h, gpost),
                (eb_h, eb), (enc_h, enc), (dec_h, dec), (gate_h, gate), (up_h, up), (d2_h, d2),
            )
        )
    ]
    for load in loads:
        load.start()

    barrier = pltpu.get_barrier_semaphore()

    @pl.loop(1, 16)
    def _(i):
        pl.semaphore_signal(barrier, inc=1, device_id=in_plane(i), device_id_type=MESH)

    @pl.loop(1, 8)
    def _(i):
        pl.semaphore_signal(barrier, inc=1, device_id=in_z(i), device_id_type=MESH)

    pl.semaphore_signal(barrier, inc=1, device_id=other, device_id_type=MESH)

    loads[0].wait()
    loads[1].wait()
    for g in range(7):
        part = jnp.dot(hid[...], d1[:, 512 * g : 512 * g + 512], preferred_element_type=F32)
        for j in range(4):
            row = 4 * (4 * g + j)
            for piece in range(8):
                parts[piece, row : row + 4, :] = part[4 * piece : 4 * piece + 4, 128 * j : 128 * j + 128]
    for piece in range(8):
        parts_b[piece] = parts[piece].astype(BF16)

    pl.semaphore_wait(barrier, 23)

    def b1(i):
        return send(parts_b.at[lax.rem(k + i, 8)], land_b1.at[i], s_b1.at[i], r_b1.at[i], in_k(i))

    @pl.loop(1, 8)
    def _(i):
        b1(i).start()

    for i in range(2, 8):
        loads[i].wait()
    for j in range(T):
        tile = slice(128 * j, 128 * j + 128)
        old = resid[:, tile].astype(F32)
        for piece in range(8):
            resid_c[piece, 4 * j : 4 * j + 4, :] = old[4 * piece : 4 * piece + 4, :]
        g1_c[4 * j : 4 * j + 4, :] = jnp.broadcast_to(g1[j : j + 1, :], (4, 128))
        db_c[4 * j : 4 * j + 4, :] = jnp.broadcast_to(db[j : j + 1, :], (4, 128))
        gpre_row[:, tile] = jnp.broadcast_to(gpre[j : j + 1, :], (8, 128))
        gpost_row[:, tile] = jnp.broadcast_to(gpost[j : j + 1, :], (8, 128))
        db_row[j // 7, :, 128 * (j % 7) : 128 * (j % 7) + 128] = jnp.broadcast_to(db[j : j + 1, :], (8, 128))
    gpost_row[:, D:] = jnp.zeros((8, 128), F32)
    clean_u[:, D:] = jnp.zeros((32, 128), F32)
    recon_u[:, D:] = jnp.zeros((32, 128), F32)
    second[:, :, 448:] = jnp.zeros((2, 32, 192), F32)
    f_src[:, :, :, 448:] = jnp.zeros((2, 8, 32, 64), BF16)
    f_own[:, :, :, 448:] = jnp.zeros((2, 8, 32, 64), F32)

    for i in range(1, 8):
        b1(i).wait_recv()
    total = parts[k]
    for i in range(1, 8):
        total += land_b1[i].astype(F32)
    send_b2[...] = total.astype(BF16)

    def b2(i):
        return send(send_b2, land_b2.at[i], s_b2.at[i], r_b2.at[i], in_z(i))

    @pl.loop(1, 8)
    def _(i):
        b2(i).start()

    for i in range(1, 8):
        b2(i).wait_recv()
    for i in range(1, 8):
        total += land_b2[i].astype(F32)
    squares = total[0:8] * total[0:8]
    for i in range(1, 14):
        squares += total[8 * i : 8 * i + 8] * total[8 * i : 8 * i + 8]
    squares += pltpu.roll(squares, 4, 0)
    scale = lax.rsqrt(jnp.sum(squares, axis=1, keepdims=True) / D + EPS)
    scale = jnp.concatenate([jnp.broadcast_to(scale, (8, 128))] * 14, axis=0)
    mine = r * 8 + k
    clean_all[mine] = (resid_c[k] + total * scale * g1_c[...]).astype(BF16)

    def spread(i):
        return send(clean_all.at[mine], clean_all.at[mine], s_c.at[i], r_c.at[i], in_plane(i))

    def arrival(i):
        source = lax.rem(m + 16 - i, 16)
        at = ((source // 8) * 2 + c) * 8 + lax.rem(source, 8)
        return send(clean_all.at[at], clean_all.at[at], s_c.at[i], r_c.at[i], in_plane(i)), at

    def forward(i, at):
        return send(clean_all.at[at], clean_all.at[at], s_cc.at[i], r_cc.at[i], other)

    @pl.loop(1, 16)
    def _(i):
        spread(i).start()

    forward(0, mine).start()

    @pl.loop(1, 16)
    def _(i):
        copy, at = arrival(i)
        copy.wait_recv()
        forward(i, at).start()

    @pl.loop(0, 16)
    def _(i):
        source = lax.rem(m + 16 - i, 16)
        at = ((source // 8) * 2 + 1 - c) * 8 + lax.rem(source, 8)
        forward(i, at).wait_recv()

    for q in range(32):
        centered = (clean_all[q].astype(F32) - db_c[...]).astype(BF16).astype(F32)
        for j in range(T):
            cent[4 * q : 4 * q + 4, 128 * j : 128 * j + 128] = centered[4 * j : 4 * j + 4, :]
    lhs[...] = cent[...].astype(BF16)
    loads[8].wait()
    pre_act = jnp.dot(lhs[...], enc[...], preferred_element_type=F32) + eb[...]
    lat[...] = jnp.maximum(pre_act, 0.0).astype(BF16)
    lat_o[...] = lat[...]

    def tokens_of(core):
        low = lat[pl.ds(pl.multiple_of(core * 32, 32), 32), :]
        high = lat[pl.ds(pl.multiple_of(core * 32 + 64, 32), 32), :]
        return jnp.concatenate([low, high], axis=0)

    def to_other(g):
        return send(pre_src.at[g], pre_land.at[g], s_p.at[g], r_p.at[g], other)

    loads[9].wait()
    theirs = tokens_of(1 - c)
    for g in range(4):
        cols = slice(896 * g, 896 * g + 896)
        pre_src[g] = jnp.dot(theirs, dec[:, cols], preferred_element_type=F32).astype(BF16)
        to_other(g).start()
    ours = tokens_of(c)

    def e1(g, to_yl, to_yh):
        to = to_yl * 8 + g * 2 + to_yh
        i = lax.rem(to + 16 - m, 16)
        row = 32 * to_yl + 16 * to_yh
        return to, send(e_src.at[g, row : row + 16, :], land_e1.at[i], s_e1.at[i], r_e1.at[i], in_plane(i))

    for g in range(4):
        cols = slice(896 * g, 896 * g + 896)
        e_own[g] = jnp.dot(ours, dec[:, cols], preferred_element_type=F32)
        to_other(g).wait_recv()
        e_own[g] += pre_land[g].astype(F32)
        e_src[g] = e_own[g].astype(BF16)
        for to_yl in range(2):
            for to_yh in range(2):
                to, copy = e1(g, to_yl, to_yh)

                @pl.when(to != m)
                def _(copy=copy):
                    copy.start()

    def layer(h, stream):
        squares = jnp.zeros((32, 128), F32)
        for j in range(T):
            tile = stream[:, 128 * j : 128 * j + 128]
            squares += tile * tile
        scale = lax.rsqrt(jnp.sum(squares, axis=1, keepdims=True) / D + EPS)
        for g in range(7):
            cols = slice(512 * g, 512 * g + 512)
            lhs_f[h, :, cols] = (stream[:, cols] * scale * gpre_row[0:1, cols]).astype(BF16)
        gate_out = lax.dot_general(lhs_f[h], gate[...], (((1,), (1,)), ((), ())), preferred_element_type=F32)
        up_out = lax.dot_general(lhs_f[h], up[...], (((1,), (1,)), ((), ())), preferred_element_type=F32)
        act = (gelu(gate_out) * up_out).astype(BF16)
        for g in range(4):
            part = jnp.dot(act, d2[:, 896 * g : 896 * g + 896], preferred_element_type=F32)
            for half in range(2):
                piece = part[:, 448 * half : 448 * half + 448]
                f_own[h, 2 * g + half, :, 0:448] = piece
                f_src[h, 2 * g + half, :, 0:448] = piece.astype(BF16)

    for q in range(8):
        clean = clean_all[r * 8 + q].astype(F32)
        for j in range(T):
            clean_u[4 * q : 4 * q + 4, 128 * j : 128 * j + 128] = clean[4 * j : 4 * j + 4, :]
    loads[10].wait()
    loads[11].wait()
    loads[12].wait()
    layer(0, clean_u)

    for i in range(1, 16):
        send(land_e1.at[i], land_e1.at[i], s_e1.at[i], r_e1.at[i], in_plane(i)).wait_recv()
    row = pl.multiple_of(32 * yl + 16 * yh, 16)
    total = e_own[x, pl.ds(row, 16), :]
    for i in range(1, 16):
        total += land_e1[i].astype(F32)
    send_e2[...] = total.astype(BF16)

    def e2(i):
        return send(send_e2, land_e2.at[i], s_e2.at[i], r_e2.at[i], in_z(i))

    @pl.loop(1, 8)
    def _(i):
        e2(i).start()

    def f1(h, i):
        return send(f_src.at[h, lax.rem(k + i, 8)], land_f1.at[h, i], s_f1.at[h, i], r_f1.at[h, i], in_k(i))

    def f2(h, i):
        return send(send_f2.at[h], land_f2.at[h, i], s_f2.at[h, i], r_f2.at[h, i], in_z(i))

    def f3(h, i):
        return send(send_f3.at[h], land_f3.at[h, i], s_f3.at[h, i], r_f3.at[h, i], in_k(i))

    @pl.loop(1, 8)
    def _(i):
        f1(0, i).start()

    for i in range(1, 8):
        e2(i).wait_recv()
    for i in range(1, 8):
        total += land_e2[i].astype(F32)
    recon_p[k] = (total + db_row[x, 0:1, :]).astype(BF16)

    def e3(i):
        return send(recon_p.at[k], recon_p.at[k], s_e3.at[i], r_e3.at[i], in_k(i))

    @pl.loop(1, 8)
    def _(i):
        e3(i).start()

    def sum_over_k(h):
        for i in range(1, 8):
            f1(h, i).wait_recv()
        total = f_own[h, k]
        for i in range(1, 8):
            total += land_f1[h, i].astype(F32)
        f_sum[h] = total
        send_f2[h] = total.astype(BF16)

        @pl.loop(1, 8)
        def _(i):
            f2(h, i).start()

    diagonal = (
        lax.broadcasted_iota(jnp.int32, (32, 128), 0) == lax.broadcasted_iota(jnp.int32, (32, 128), 1)
    ).astype(F32)

    def sum_over_z(h):
        for i in range(1, 8):
            f2(h, i).wait_recv()
        total = f_sum[h]
        for i in range(1, 8):
            total += land_f2[h, i].astype(F32)
        second[h, :, 0:512] = total
        squares = jnp.sum(total * total, axis=1, keepdims=True)
        flat = jnp.sum(squares * diagonal, axis=0, keepdims=True)
        send_f3[h] = jnp.broadcast_to(flat, (8, 128))

        @pl.loop(1, 8)
        def _(i):
            f3(h, i).start()

    def outputs(h, stream):
        for i in range(1, 8):
            f3(h, i).wait_recv()
        flat = send_f3[h]
        for i in range(1, 8):
            flat += land_f3[h, i]
        squares = jnp.sum(flat[0:1, :] * diagonal, axis=1, keepdims=True)
        gain = pick(gpost_row, 56 * s, 8)[0:1, :]
        return pick(stream, 56 * s, 32) + pick(second.at[h], 56 * z, 32) * lax.rsqrt(squares / D + EPS) * gain

    sum_over_k(0)

    def arrived(i):
        at = lax.rem(k + 8 - i, 8)
        return send(recon_p.at[at], recon_p.at[at], s_e3.at[i], r_e3.at[i], in_k(i))

    for i in range(1, 8):
        arrived(i).wait_recv()
    for q in range(8):
        row, col = 16 * (q % 2), 896 * (q // 2)
        recon_u[row : row + 16, col : col + 896] = recon_p[q].astype(F32)
    layer(1, recon_u)

    @pl.loop(1, 8)
    def _(i):
        f1(1, i).start()

    sum_over_z(0)
    sum_over_k(1)
    clean_out = outputs(0, clean_u)
    sum_over_z(1)
    delta_o[...] = outputs(1, recon_u) - clean_out

    @pl.loop(1, 8)
    def _(i):
        b1(i).wait_send()
        b2(i).wait_send()
        e2(i).wait_send()
        e3(i).wait_send()
        for h in range(2):
            f1(h, i).wait_send()
            f2(h, i).wait_send()
            f3(h, i).wait_send()

    @pl.loop(1, 16)
    def _(i):
        spread(i).wait_send()
        send(land_e1.at[i], land_e1.at[i], s_e1.at[i], r_e1.at[i], in_plane(i)).wait_send()

    @pl.loop(0, 16)
    def _(i):
        forward(i, mine).wait_send()

    for g in range(4):
        to_other(g).wait_send()


def on_device(
    hidden_in, resid, down_one, gain_one, enc_weight, enc_bias, dec_weight, dec_bias, gain_pre, gate_two, up_two,
    down_two, gain_post,
):
    tiles = (T, 128)
    args = (
        hidden_in, resid, down_one, gain_one.reshape(tiles), enc_weight, enc_bias.reshape(1, 256), dec_weight,
        dec_bias.reshape(tiles), gain_pre.reshape(tiles), gate_two.T, up_two.T, down_two,
        gain_post.reshape(tiles),
    )
    dma = pltpu.SemaphoreType.DMA
    vmem = pltpu.VMEM
    latents, delta = pl.pallas_call(
        kernel,
        name="spliced",
        out_shape=(vmem((128, 256), BF16), vmem((32, 128), F32)),
        in_specs=[pl.BlockSpec(memory_space=pl.ANY)] * len(args),
        out_specs=[pl.BlockSpec(memory_space=pltpu.VMEM)] * 2,
        scratch_shapes=[vmem(a.shape, a.dtype) for a in args]
        + [
            vmem((8, 112, 128), F32),
            vmem((8, 112, 128), BF16),
            vmem((8, 112, 128), BF16),
            vmem((112, 128), BF16),
            vmem((8, 112, 128), BF16),
            vmem((8, 112, 128), F32),
            vmem((112, 128), F32),
            vmem((112, 128), F32),
            vmem((4, 8, 896), F32),
            vmem((8, D), F32),
            vmem((8, D + 128), F32),
            vmem((32, 112, 128), BF16),
            vmem((128, D), F32),
            vmem((128, D), BF16),
            vmem((128, 256), BF16),
            vmem((4, 64, 896), BF16),
            vmem((4, 64, 896), BF16),
            vmem((4, 64, 896), BF16),
            vmem((4, 64, 896), F32),
            vmem((16, 16, 896), BF16),
            vmem((16, 896), BF16),
            vmem((8, 16, 896), BF16),
            vmem((8, 16, 896), BF16),
            vmem((32, D + 128), F32),
            vmem((32, D + 128), F32),
            vmem((2, 32, D), BF16),
            vmem((2, 8, 32, 512), BF16),
            vmem((2, 8, 32, 512), F32),
            vmem((2, 8, 32, 512), BF16),
            vmem((2, 32, 512), F32),
            vmem((2, 32, 512), BF16),
            vmem((2, 8, 32, 512), BF16),
            vmem((2, 32, 640), F32),
            vmem((2, 8, 128), F32),
            vmem((2, 8, 8, 128), F32),
            dma((13,)),
            dma((8,)), dma((8,)), dma((8,)), dma((8,)),
            dma((16,)), dma((16,)), dma((16,)), dma((16,)),
            dma((4,)), dma((4,)), dma((16,)), dma((16,)),
            dma((8,)), dma((8,)), dma((8,)), dma((8,)),
            dma((2, 8)), dma((2, 8)), dma((2, 8)), dma((2, 8)), dma((2, 8)), dma((2, 8)),
        ],
        compiler_params=pltpu.CompilerParams(
            collective_id=0, has_side_effects=True, vmem_limit_bytes=62 * 2**20
        ),
        cost_estimate=pl.CostEstimate(flops=10**9, bytes_accessed=12 * 10**6, transcendentals=10**5),
    )(*args)
    return latents, delta[:, :56]


def solution(mesh):
    in_specs = (
        P("rows", "shard"),
        P("rows", None),
        P("shard", None),
        P(),
        P(None, ("rows", "shard")),
        P(("rows", "shard")),
        P(("rows", "shard"), None),
        P(),
        P(),
        P(None, "shard"),
        P(None, "shard"),
        P("shard", None),
        P(),
    )
    out_specs = (P(None, ("rows", "shard")), P("rows", "shard"))
    return jax.shard_map(on_device, mesh=mesh, in_specs=in_specs, out_specs=out_specs, check_vma=False)
```

```python
import functools

import jax
import jax.numpy as jnp
from jax import lax
from jax.experimental import pallas as pl
from jax.experimental.pallas import tpu as pltpu
from jax.sharding import PartitionSpec as P

D = 3584
T = D // 128
MESH = pl.DeviceIdType.MESH
F32, BF16 = jnp.float32, jnp.bfloat16
EPS = 1e-06


def pick(ref, start, rows):
    tile, turn = start // 128, lax.rem(start, 128)
    lo = ref[0:rows, pl.ds(pl.multiple_of(tile * 128, 128), 128)]
    hi = ref[0:rows, pl.ds(pl.multiple_of(tile * 128 + 128, 128), 128)]
    shift = lax.rem(128 - turn, 128)
    lane = lax.broadcasted_iota(jnp.int32, (rows, 128), 1)
    return jnp.where(lane < 128 - turn, pltpu.roll(lo, shift, 1), pltpu.roll(hi, shift, 1))


def around(t, n):
    return lax.rem(n // 2 + n + (1 - 2 * lax.rem(t, 2)) * ((t + 1) // 2), n)


def gelu(v):
    return 0.5 * v * (1.0 + jnp.tanh(0.7978845608028654 * (v + 0.044715 * (v * v * v))))


def kernel(
    hid_h, resid_h, d1_h, g1_h, enc_h, eb_h, dec_h, db_h, gpre_h, gate_h, up_h, d2_h, gpost_h,
    lat_o, delta_o,
    hid, resid, d1, g1, enc, eb, dec, db, gpre, gate, up, d2, gpost,
    parts, parts_b, land_b1, send_b2, land_b2, resid_c, g1_c, db_c, db_row, gpre_row, gpost_row,
    clean_all, cent, lhs, lat, pre_src, pre_land, e_src, e_own, land_e1, send_e2, land_e2, recon_p,
    clean_u, recon_u, lhs_f, f_src, f_own, land_f1, f_sum, send_f2, land_f2, second, send_f3, land_f3,
    load_sem, s_b1, r_b1, s_b2, r_b2, s_c, r_c, s_cc, r_cc, s_p, r_p, s_e1, r_e1, s_e2, r_e2, s_e3, r_e3,
    s_f1, r_f1, s_f2, r_f2, s_f3, r_f3,
):
    r = lax.axis_index("rows")
    s = lax.axis_index("shard")
    yl, c = r // 2, lax.rem(r, 2)
    k, z = s // 8, lax.rem(s, 8)
    x, yh = k // 2, lax.rem(k, 2)
    y = 2 * yh + yl
    other = (yl * 2 + 1 - c, s)

    def k_at(t):
        return lax.rem(x + around(t // 2, 4), 4) * 2 + lax.rem(yh + 1 - lax.rem(t, 2), 2)

    def k_from(t):
        return lax.rem(x + 4 - around(t // 2, 4), 4) * 2 + lax.rem(yh + 1 - lax.rem(t, 2), 2)

    def in_k(t):
        return (r, k_at(t) * 8 + z)

    def in_z(t):
        return (r, k * 8 + lax.rem(z + around(t, 8), 8))

    def plane_at(to_x, to_y):
        return (lax.rem(to_y, 2) * 2 + c, (to_x * 2 + to_y // 2) * 8 + z)

    def in_plane(t):
        return plane_at(lax.rem(x + around(t // 4, 4), 4), lax.rem(y + around(lax.rem(t, 4), 4), 4))

    def chunk_from(t, core):
        from_x = lax.rem(x + 4 - around(t // 4, 4), 4)
        from_y = lax.rem(y + 4 - around(lax.rem(t, 4), 4), 4)
        return (lax.rem(from_y, 2) * 2 + core) * 8 + from_x * 2 + from_y // 2

    def send(src, dst, s_sem, r_sem, device):
        return pltpu.make_async_remote_copy(
            src_ref=src, dst_ref=dst, send_sem=s_sem, recv_sem=r_sem, device_id=device, device_id_type=MESH
        )

    loads = [
        pltpu.make_async_copy(a, b, load_sem.at[i])
        for i, (a, b) in enumerate(
            (
                (hid_h, hid), (d1_h, d1), (resid_h, resid), (g1_h, g1), (db_h, db), (gpre_h, gpre), (gpost_h, gpost),
                (eb_h, eb), (enc_h, enc), (dec_h, dec), (gate_h, gate), (up_h, up), (d2_h, d2),
            )
        )
    ]
    for load in loads:
        load.start()

    barrier = pltpu.get_barrier_semaphore()

    @pl.loop(0, 15)
    def _(t):
        pl.semaphore_signal(barrier, inc=1, device_id=in_plane(t), device_id_type=MESH)

    @pl.loop(0, 7)
    def _(t):
        pl.semaphore_signal(barrier, inc=1, device_id=in_z(t), device_id_type=MESH)

    pl.semaphore_signal(barrier, inc=1, device_id=other, device_id_type=MESH)

    loads[0].wait()
    loads[1].wait()
    for g in range(7):
        part = jnp.dot(hid[...], d1[:, 512 * g : 512 * g + 512], preferred_element_type=F32)
        for j in range(4):
            row = 4 * (4 * g + j)
            for piece in range(8):
                parts[piece, row : row + 4, :] = part[4 * piece : 4 * piece + 4, 128 * j : 128 * j + 128]
    for piece in range(8):
        parts_b[piece] = parts[piece].astype(BF16)

    pl.semaphore_wait(barrier, 23)

    halves = ((0, 64), (64, 48))

    def b1(h, t):
        rows = pl.ds(*halves[h])
        return send(
            parts_b.at[k_at(t), rows, :], land_b1.at[t, rows, :], s_b1.at[h, t], r_b1.at[h, t], in_k(t)
        )

    for h in range(2):

        @pl.loop(0, 7)
        def _(t, h=h):
            b1(h, t).start()

    for i in range(2, 8):
        loads[i].wait()
    for j in range(T):
        tile = slice(128 * j, 128 * j + 128)
        old = resid[:, tile].astype(F32)
        for piece in range(8):
            resid_c[piece, 4 * j : 4 * j + 4, :] = old[4 * piece : 4 * piece + 4, :]
        g1_c[4 * j : 4 * j + 4, :] = jnp.broadcast_to(g1[j : j + 1, :], (4, 128))
        db_c[4 * j : 4 * j + 4, :] = jnp.broadcast_to(db[j : j + 1, :], (4, 128))
        gpre_row[:, tile] = jnp.broadcast_to(gpre[j : j + 1, :], (8, 128))
        gpost_row[:, tile] = jnp.broadcast_to(gpost[j : j + 1, :], (8, 128))
        db_row[j // 7, :, 128 * (j % 7) : 128 * (j % 7) + 128] = jnp.broadcast_to(db[j : j + 1, :], (8, 128))
    gpost_row[:, D:] = jnp.zeros((8, 128), F32)
    clean_u[:, D:] = jnp.zeros((32, 128), F32)
    recon_u[:, D:] = jnp.zeros((32, 128), F32)
    second[:, :, 448:] = jnp.zeros((2, 32, 192), F32)
    f_src[:, :, :, 448:] = jnp.zeros((2, 8, 32, 64), BF16)
    f_own[:, :, :, 448:] = jnp.zeros((2, 8, 32, 64), F32)

    def b2(h, t):
        rows = pl.ds(*halves[h])
        return send(send_b2.at[rows, :], land_b2.at[t, rows, :], s_b2.at[h, t], r_b2.at[h, t], in_z(t))

    sums = []
    for h, (low, count) in enumerate(halves):
        for t in range(7):
            b1(h, t).wait_recv()
        total = parts[k, low : low + count, :]
        for t in range(7):
            total += land_b1[t, low : low + count, :].astype(F32)
        send_b2[low : low + count, :] = total.astype(BF16)

        @pl.loop(0, 7)
        def _(t, h=h):
            b2(h, t).start()

        sums.append(total)

    for h, (low, count) in enumerate(halves):
        for t in range(7):
            b2(h, t).wait_recv()
        for t in range(7):
            sums[h] += land_b2[t, low : low + count, :].astype(F32)
    total = jnp.concatenate(sums, axis=0)
    squares = total[0:8] * total[0:8]
    for i in range(1, 14):
        squares += total[8 * i : 8 * i + 8] * total[8 * i : 8 * i + 8]
    squares += pltpu.roll(squares, 4, 0)
    scale = lax.rsqrt(jnp.sum(squares, axis=1, keepdims=True) / D + EPS)
    scale = jnp.concatenate([jnp.broadcast_to(scale, (8, 128))] * 14, axis=0)
    mine = r * 8 + k
    clean_all[mine] = (resid_c[k] + total * scale * g1_c[...]).astype(BF16)

    def spread(t):
        return send(clean_all.at[mine], clean_all.at[mine], s_c.at[t], r_c.at[t], in_plane(t))

    def forward(t, at):
        return send(clean_all.at[at], clean_all.at[at], s_cc.at[t], r_cc.at[t], other)

    def place(core):
        @pl.loop(0, 2)
        def _(low):
            group = low * 2 + core
            for q in range(8):
                centered = (clean_all[group * 8 + q].astype(F32) - db_c[...]).astype(BF16).astype(F32)
                for j in range(T):
                    cent[group, 4 * q : 4 * q + 4, 128 * j : 128 * j + 128] = centered[4 * j : 4 * j + 4, :]
            lhs[pl.ds(pl.multiple_of(group * 32, 32), 32), :] = cent[group].astype(BF16)

    @pl.loop(0, 15)
    def _(t):
        spread(t).start()

    forward(15, mine).start()

    @pl.loop(0, 15)
    def _(i):
        t = 14 - i
        at = chunk_from(t, c)
        send(clean_all.at[at], clean_all.at[at], s_c.at[t], r_c.at[t], in_plane(t)).wait_recv()
        forward(t, at).start()

    place(c)

    @pl.loop(0, 16)
    def _(i):
        t = 15 - i
        at = chunk_from(t, 1 - c)
        forward(t, at).wait_recv()

    place(1 - c)
    loads[8].wait()
    pre_act = jnp.dot(lhs[...], enc[...], preferred_element_type=F32) + eb[...]
    lat[...] = jnp.maximum(pre_act, 0.0).astype(BF16)
    lat_o[...] = lat[...]

    cuts = ((0, 512), (512, 384))

    def tokens_of(core):
        low = lat[pl.ds(pl.multiple_of(core * 32, 32), 32), :]
        high = lat[pl.ds(pl.multiple_of(core * 32 + 64, 32), 32), :]
        return jnp.concatenate([low, high], axis=0)

    def decoded(tokens, g, h):
        first_col = lax.rem(x + around(jnp.int32(g), 4), 4) * 896 + cuts[h][0]
        cols = pl.ds(pl.multiple_of(first_col, 128), cuts[h][1])
        return jnp.dot(tokens, dec[:, cols], preferred_element_type=F32)

    def to_other(h, g):
        cols = pl.ds(*cuts[h])
        return send(pre_src.at[g, :, cols], pre_land.at[g, :, cols], s_p.at[h, g], r_p.at[h, g], other)

    loads[9].wait()
    theirs = tokens_of(1 - c)
    for h, (low, count) in enumerate(cuts):
        for g in range(4):
            pre_src[g, :, low : low + count] = decoded(theirs, g, h).astype(BF16)
            to_other(h, g).start()
    ours = tokens_of(c)

    def e1(h, t):
        to_x, to_y = lax.rem(x + around(t // 4, 4), 4), lax.rem(y + around(lax.rem(t, 4), 4), 4)
        rows = pl.ds(pl.multiple_of(32 * lax.rem(to_y, 2) + 16 * (to_y // 2), 16), 16)
        cols = pl.ds(*cuts[h])
        return send(
            e_src.at[t // 4, rows, cols], land_e1.at[t, :, cols], s_e1.at[h, t], r_e1.at[h, t], plane_at(to_x, to_y)
        )

    for h, (low, count) in enumerate(cuts):
        for g in range(4):
            own = decoded(ours, g, h)
            to_other(h, g).wait_recv()
            own += pre_land[g, :, low : low + count].astype(F32)
            if g == 3:
                e_own[:, low : low + count] = own
            e_src[g, :, low : low + count] = own.astype(BF16)

            @pl.loop(4 * g, min(4 * g + 4, 15))
            def _(t, h=h):
                e1(h, t).start()

    def layer(h, stream):
        squares = jnp.zeros((32, 128), F32)
        for j in range(T):
            tile = stream[:, 128 * j : 128 * j + 128]
            squares += tile * tile
        scale = lax.rsqrt(jnp.sum(squares, axis=1, keepdims=True) / D + EPS)
        for g in range(7):
            cols = slice(512 * g, 512 * g + 512)
            lhs_f[h, :, cols] = (stream[:, cols] * scale * gpre_row[0:1, cols]).astype(BF16)
        gate_out = lax.dot_general(lhs_f[h], gate[...], (((1,), (1,)), ((), ())), preferred_element_type=F32)
        up_out = lax.dot_general(lhs_f[h], up[...], (((1,), (1,)), ((), ())), preferred_element_type=F32)
        act = (gelu(gate_out) * up_out).astype(BF16)
        for g in range(4):
            part = jnp.dot(act, d2[:, 896 * g : 896 * g + 896], preferred_element_type=F32)
            for half in range(2):
                piece = part[:, 448 * half : 448 * half + 448]
                f_own[h, 2 * g + half, :, 0:448] = piece
                f_src[h, 2 * g + half, :, 0:448] = piece.astype(BF16)

    for q in range(8):
        clean = clean_all[r * 8 + q].astype(F32)
        for j in range(T):
            clean_u[4 * q : 4 * q + 4, 128 * j : 128 * j + 128] = clean[4 * j : 4 * j + 4, :]
    loads[10].wait()
    loads[11].wait()
    loads[12].wait()
    layer(0, clean_u)

    row = pl.multiple_of(32 * yl + 16 * yh, 16)

    def e2(h, t):
        cols = pl.ds(*cuts[h])
        return send(send_e2.at[:, cols], land_e2.at[t, :, cols], s_e2.at[h, t], r_e2.at[h, t], in_z(t))

    def e3(h, t, at):
        cols = pl.ds(*cuts[h])
        return send(recon_p.at[at, :, cols], recon_p.at[at, :, cols], s_e3.at[h, t], r_e3.at[h, t], in_k(t))

    def f1(h, q, t):
        rows = pl.ds(16 * q, 16)
        return send(
            f_src.at[h, k_at(t), rows, :], land_f1.at[h, t, rows, :], s_f1.at[h, q, t], r_f1.at[h, q, t], in_k(t)
        )

    def f2(h, q, t):
        rows = pl.ds(16 * q, 16)
        return send(
            send_f2.at[h, rows, :], land_f2.at[h, t, rows, :], s_f2.at[h, q, t], r_f2.at[h, q, t], in_z(t)
        )

    def f3(h, t):
        return send(send_f3.at[h], land_f3.at[h, t], s_f3.at[h, t], r_f3.at[h, t], in_k(t))

    def start_f1(h):
        for q in range(2):

            @pl.loop(0, 7)
            def _(t, q=q):
                f1(h, q, t).start()

    sums = []
    for h, (low, count) in enumerate(cuts):
        for t in range(15):
            e1(h, t).wait_recv()
        total = e_own[pl.ds(row, 16), low : low + count]
        for t in range(15):
            total += land_e1[t, :, low : low + count].astype(F32)
        send_e2[:, low : low + count] = total.astype(BF16)

        @pl.loop(0, 7)
        def _(t, h=h):
            e2(h, t).start()

        sums.append(total)

    start_f1(0)

    for h, (low, count) in enumerate(cuts):
        for t in range(7):
            e2(h, t).wait_recv()
        for t in range(7):
            sums[h] += land_e2[t, :, low : low + count].astype(F32)
        recon_p[k, :, low : low + count] = (sums[h] + db_row[x, 0:1, low : low + count]).astype(BF16)

        @pl.loop(0, 7)
        def _(t, h=h):
            e3(h, t, k).start()

    def sum_over_k(h):
        for q in range(2):
            rows = slice(16 * q, 16 * q + 16)
            for t in range(7):
                f1(h, q, t).wait_recv()
            total = f_own[h, k, rows, :]
            for t in range(7):
                total += land_f1[h, t, rows, :].astype(F32)
            f_sum[h, rows, :] = total
            send_f2[h, rows, :] = total.astype(BF16)

            @pl.loop(0, 7)
            def _(t, q=q):
                f2(h, q, t).start()

    diagonal = (
        lax.broadcasted_iota(jnp.int32, (32, 128), 0) == lax.broadcasted_iota(jnp.int32, (32, 128), 1)
    ).astype(F32)

    def sum_over_z(h):
        for q in range(2):
            for t in range(7):
                f2(h, q, t).wait_recv()
        total = f_sum[h]
        for t in range(7):
            total += land_f2[h, t].astype(F32)
        second[h, :, 0:512] = total
        squares = jnp.sum(total * total, axis=1, keepdims=True)
        flat = jnp.sum(squares * diagonal, axis=0, keepdims=True)
        send_f3[h] = jnp.broadcast_to(flat, (8, 128))

        @pl.loop(0, 7)
        def _(t):
            f3(h, t).start()

    def outputs(h, stream):
        for t in range(7):
            f3(h, t).wait_recv()
        flat = send_f3[h]
        for t in range(7):
            flat += land_f3[h, t]
        squares = jnp.sum(flat[0:1, :] * diagonal, axis=1, keepdims=True)
        gain = pick(gpost_row, 56 * s, 8)[0:1, :]
        return pick(stream, 56 * s, 32) + pick(second.at[h], 56 * z, 32) * lax.rsqrt(squares / D + EPS) * gain

    sum_over_k(0)

    for h in range(2):
        for t in range(7):
            e3(h, t, k_from(t)).wait_recv()
    for q in range(8):
        row, col = 16 * (q % 2), 896 * (q // 2)
        recon_u[row : row + 16, col : col + 896] = recon_p[q].astype(F32)
    layer(1, recon_u)

    start_f1(1)

    sum_over_z(0)
    sum_over_k(1)
    clean_out = outputs(0, clean_u)
    sum_over_z(1)
    delta_o[...] = outputs(1, recon_u) - clean_out

    @pl.loop(0, 7)
    def _(t):
        for h in range(2):
            b1(h, t).wait_send()
            b2(h, t).wait_send()
            e2(h, t).wait_send()
            e3(h, t, k).wait_send()
            f3(h, t).wait_send()
            for q in range(2):
                f1(h, q, t).wait_send()
                f2(h, q, t).wait_send()

    @pl.loop(0, 15)
    def _(t):
        spread(t).wait_send()
        for h in range(2):
            e1(h, t).wait_send()

    @pl.loop(0, 16)
    def _(t):
        forward(t, mine).wait_send()

    for h in range(2):
        for g in range(4):
            to_other(h, g).wait_send()


def on_device(
    hidden_in, resid, down_one, gain_one, enc_weight, enc_bias, dec_weight, dec_bias, gain_pre, gate_two, up_two,
    down_two, gain_post,
):
    tiles = (T, 128)
    args = (
        hidden_in, resid, down_one, gain_one.reshape(tiles), enc_weight, enc_bias.reshape(1, 256), dec_weight,
        dec_bias.reshape(tiles), gain_pre.reshape(tiles), gate_two.T, up_two.T, down_two,
        gain_post.reshape(tiles),
    )
    dma = pltpu.SemaphoreType.DMA
    vmem = pltpu.VMEM
    latents, delta = pl.pallas_call(
        kernel,
        name="spliced",
        out_shape=(vmem((128, 256), BF16), vmem((32, 128), F32)),
        in_specs=[pl.BlockSpec(memory_space=pl.ANY)] * len(args),
        out_specs=[pl.BlockSpec(memory_space=pltpu.VMEM)] * 2,
        scratch_shapes=[vmem(a.shape, a.dtype) for a in args]
        + [
            vmem((8, 112, 128), F32),
            vmem((8, 112, 128), BF16),
            vmem((8, 112, 128), BF16),
            vmem((112, 128), BF16),
            vmem((8, 112, 128), BF16),
            vmem((8, 112, 128), F32),
            vmem((112, 128), F32),
            vmem((112, 128), F32),
            vmem((4, 8, 896), F32),
            vmem((8, D), F32),
            vmem((8, D + 128), F32),
            vmem((32, 112, 128), BF16),
            vmem((4, 32, D), F32),
            vmem((128, D), BF16),
            vmem((128, 256), BF16),
            vmem((4, 64, 896), BF16),
            vmem((4, 64, 896), BF16),
            vmem((4, 64, 896), BF16),
            vmem((64, 896), F32),
            vmem((16, 16, 896), BF16),
            vmem((16, 896), BF16),
            vmem((8, 16, 896), BF16),
            vmem((8, 16, 896), BF16),
            vmem((32, D + 128), F32),
            vmem((32, D + 128), F32),
            vmem((2, 32, D), BF16),
            vmem((2, 8, 32, 512), BF16),
            vmem((2, 8, 32, 512), F32),
            vmem((2, 8, 32, 512), BF16),
            vmem((2, 32, 512), F32),
            vmem((2, 32, 512), BF16),
            vmem((2, 8, 32, 512), BF16),
            vmem((2, 32, 640), F32),
            vmem((2, 8, 128), F32),
            vmem((2, 8, 8, 128), F32),
            dma((13,)),
            dma((2, 7)), dma((2, 7)), dma((2, 7)), dma((2, 7)),
            dma((15,)), dma((15,)), dma((16,)), dma((16,)),
            dma((2, 4)), dma((2, 4)), dma((2, 15)), dma((2, 15)),
            dma((2, 7)), dma((2, 7)), dma((2, 7)), dma((2, 7)),
            dma((2, 2, 7)), dma((2, 2, 7)), dma((2, 2, 7)), dma((2, 2, 7)), dma((2, 7)), dma((2, 7)),
        ],
        compiler_params=pltpu.CompilerParams(
            collective_id=0, has_side_effects=True, vmem_limit_bytes=62 * 2**20
        ),
        cost_estimate=pl.CostEstimate(flops=10**9, bytes_accessed=12 * 10**6, transcendentals=10**5),
    )(*args)
    return latents, delta[:, :56]


def solution(mesh):
    in_specs = (
        P("rows", "shard"),
        P("rows", None),
        P("shard", None),
        P(),
        P(None, ("rows", "shard")),
        P(("rows", "shard")),
        P(("rows", "shard"), None),
        P(),
        P(),
        P(None, "shard"),
        P(None, "shard"),
        P("shard", None),
        P(),
    )
    out_specs = (P(None, ("rows", "shard")), P("rows", "shard"))
    return jax.shard_map(on_device, mesh=mesh, in_specs=in_specs, out_specs=out_specs, check_vma=False)
```

```python
import functools

import jax
import jax.numpy as jnp
from jax import lax
from jax.experimental import pallas as pl
from jax.experimental.pallas import tpu as pltpu
from jax.sharding import PartitionSpec as P

D = 3584
T = D // 128
MESH = pl.DeviceIdType.MESH
F32, BF16 = jnp.float32, jnp.bfloat16
EPS = 1e-06


def pick(ref, start, rows):
    tile, turn = start // 128, lax.rem(start, 128)
    lo = ref[0:rows, pl.ds(pl.multiple_of(tile * 128, 128), 128)]
    hi = ref[0:rows, pl.ds(pl.multiple_of(tile * 128 + 128, 128), 128)]
    shift = lax.rem(128 - turn, 128)
    lane = lax.broadcasted_iota(jnp.int32, (rows, 128), 1)
    return jnp.where(lane < 128 - turn, pltpu.roll(lo, shift, 1), pltpu.roll(hi, shift, 1))


def around(t, n):
    return lax.rem(n // 2 + n + (1 - 2 * lax.rem(t, 2)) * ((t + 1) // 2), n)


def gelu(v):
    return 0.5 * v * (1.0 + jnp.tanh(0.7978845608028654 * (v + 0.044715 * (v * v * v))))


def kernel(
    hid_h, resid_h, d1_h, g1_h, enc_h, eb_h, dec_h, db_h, gpre_h, gate_h, up_h, d2_h, gpost_h,
    lat_o, delta_o,
    hid, resid, d1, g1, enc, eb, dec, db, gpre, gate, up, d2, gpost,
    parts, parts_b, land_b1, send_b2, land_b2, resid_c, g1_c, db_c, db_row, gpre_row, gpost_row,
    clean_all, cent, lhs, lat, lat_src, lat_land, e_src, e_own, land_e1, send_e2, land_e2, recon_p,
    clean_u, recon_u, lhs_f, f_src, f_own, land_f1, f_sum, send_f2, land_f2, second, send_f3, land_f3,
    d1_sem, load_sem, s_b1, r_b1, s_b2, r_b2, s_w, r_w, s_c, r_c, s_l, r_l, s_e1, r_e1, s_e2, r_e2, s_e3, r_e3,
    s_f1, r_f1, s_f2, r_f2, s_f3, r_f3,
):
    r = lax.axis_index("rows")
    s = lax.axis_index("shard")
    yl, c = r // 2, lax.rem(r, 2)
    k, z = s // 8, lax.rem(s, 8)
    x, yh = k // 2, lax.rem(k, 2)
    y, m = 2 * yh + yl, yl * 8 + k
    other = (yl * 2 + 1 - c, s)

    def k_at(t):
        return lax.rem(x + around(t // 2, 4), 4) * 2 + lax.rem(yh + 1 - lax.rem(t, 2), 2)

    def k_from(t):
        return lax.rem(x + 4 - around(t // 2, 4), 4) * 2 + lax.rem(yh + 1 - lax.rem(t, 2), 2)

    def in_k(t):
        return (r, k_at(t) * 8 + z)

    def in_z(t):
        return (r, k * 8 + lax.rem(z + around(t, 8), 8))

    def plane_at(to_x, to_y):
        return (lax.rem(to_y, 2) * 2 + c, (to_x * 2 + to_y // 2) * 8 + z)

    def in_plane(t):
        return plane_at(lax.rem(x + around(t // 4, 4), 4), lax.rem(y + around(lax.rem(t, 4), 4), 4))

    def chunk_from(t):
        from_x = lax.rem(x + 4 - around(t // 4, 4), 4)
        from_y = lax.rem(y + 4 - around(lax.rem(t, 4), 4), 4)
        return lax.rem(from_y, 2) * 8 + from_x * 2 + from_y // 2

    def send(src, dst, s_sem, r_sem, device):
        return pltpu.make_async_remote_copy(
            src_ref=src, dst_ref=dst, send_sem=s_sem, recv_sem=r_sem, device_id=device, device_id_type=MESH
        )

    def first_load(g):
        cols = pl.ds(512 * g, 512)
        return pltpu.make_async_copy(d1_h.at[:, cols], d1.at[:, cols], d1_sem.at[g])

    loads = [
        pltpu.make_async_copy(a, b, load_sem.at[i])
        for i, (a, b) in enumerate(
            (
                (hid_h, hid), (resid_h, resid), (g1_h, g1), (db_h, db), (gpre_h, gpre), (gpost_h, gpost),
                (eb_h, eb.at[:, pl.ds(0, 256)]), (enc_h, enc.at[:, pl.ds(0, 256)]), (dec_h, dec.at[pl.ds(0, 256), :]),
                (gate_h, gate), (up_h, up), (d2_h, d2),
            )
        )
    ]
    loads[0].start()
    for g in range(7):
        first_load(g).start()

    barrier = pltpu.get_barrier_semaphore()

    @pl.loop(0, 15)
    def _(t):
        pl.semaphore_signal(barrier, inc=1, device_id=in_plane(t), device_id_type=MESH)

    @pl.loop(0, 7)
    def _(t):
        pl.semaphore_signal(barrier, inc=1, device_id=in_z(t), device_id_type=MESH)

    pl.semaphore_signal(barrier, inc=1, device_id=other, device_id_type=MESH)

    thirds = ((0, 32), (32, 32), (64, 48))

    def b1(h, t):
        rows = pl.ds(*thirds[h])
        return send(
            parts_b.at[k_at(t), rows, :], land_b1.at[t, rows, :], s_b1.at[h, t], r_b1.at[h, t], in_k(t)
        )

    loads[0].wait()
    for g in range(7):
        first_load(g).wait()
        part = jnp.dot(hid[...], d1[:, 512 * g : 512 * g + 512], preferred_element_type=F32)
        for j in range(4):
            row = 4 * (4 * g + j)
            for piece in range(8):
                parts[piece, row : row + 4, :] = part[4 * piece : 4 * piece + 4, 128 * j : 128 * j + 128]
        if g in (1, 3, 6):
            h = (1, 3, 6).index(g)
            rows = slice(thirds[h][0], sum(thirds[h]))
            for piece in range(8):
                parts_b[piece, rows, :] = parts[piece, rows, :].astype(BF16)
            if h == 0:
                pl.semaphore_wait(barrier, 23)

            @pl.loop(0, 7)
            def _(t, h=h):
                b1(h, t).start()

    for load in loads[1:]:
        load.start()
    shared = [
        send(a, b, s_w.at[i], r_w.at[i], other)
        for i, (a, b) in enumerate(
            (
                (eb_h, eb.at[:, pl.ds(256, 256)]),
                (enc_h, enc.at[:, pl.ds(256, 256)]),
                (dec_h, dec.at[pl.ds(256, 256), :]),
            )
        )
    ]
    for share in shared:
        share.start()

    for i in range(1, 7):
        loads[i].wait()
    for j in range(T):
        tile = slice(128 * j, 128 * j + 128)
        old = resid[:, tile].astype(F32)
        for piece in range(8):
            resid_c[piece, 4 * j : 4 * j + 4, :] = old[4 * piece : 4 * piece + 4, :]
        g1_c[4 * j : 4 * j + 4, :] = jnp.broadcast_to(g1[j : j + 1, :], (4, 128))
        db_c[4 * j : 4 * j + 4, :] = jnp.broadcast_to(db[j : j + 1, :], (4, 128))
        gpre_row[:, tile] = jnp.broadcast_to(gpre[j : j + 1, :], (8, 128))
        gpost_row[:, tile] = jnp.broadcast_to(gpost[j : j + 1, :], (8, 128))
        db_row[j // 7, :, 128 * (j % 7) : 128 * (j % 7) + 128] = jnp.broadcast_to(db[j : j + 1, :], (8, 128))
    gpost_row[:, D:] = jnp.zeros((8, 128), F32)
    clean_u[:, D:] = jnp.zeros((32, 128), F32)
    recon_u[:, D:] = jnp.zeros((32, 128), F32)
    second[:, :, 448:] = jnp.zeros((2, 32, 192), F32)
    f_src[:, :, :, 448:] = jnp.zeros((2, 8, 32, 64), BF16)
    f_own[:, :, :, 448:] = jnp.zeros((2, 8, 32, 64), F32)

    def b2(h, t):
        rows = pl.ds(*thirds[h])
        return send(send_b2.at[rows, :], land_b2.at[t, rows, :], s_b2.at[h, t], r_b2.at[h, t], in_z(t))

    sums = []
    for h, (low, count) in enumerate(thirds):
        for t in range(7):
            b1(h, t).wait_recv()
        total = parts[k, low : low + count, :]
        for t in range(7):
            total += land_b1[t, low : low + count, :].astype(F32)
        send_b2[low : low + count, :] = total.astype(BF16)

        @pl.loop(0, 7)
        def _(t, h=h):
            b2(h, t).start()

        sums.append(total)

    for h, (low, count) in enumerate(thirds):
        for t in range(7):
            b2(h, t).wait_recv()
        for t in range(7):
            sums[h] += land_b2[t, low : low + count, :].astype(F32)
    total = jnp.concatenate(sums, axis=0)
    squares = total[0:8] * total[0:8]
    for i in range(1, 14):
        squares += total[8 * i : 8 * i + 8] * total[8 * i : 8 * i + 8]
    squares += pltpu.roll(squares, 4, 0)
    scale = lax.rsqrt(jnp.sum(squares, axis=1, keepdims=True) / D + EPS)
    scale = jnp.concatenate([jnp.broadcast_to(scale, (8, 128))] * 14, axis=0)
    clean_all[m] = (resid_c[k] + total * scale * g1_c[...]).astype(BF16)

    def spread(t):
        return send(clean_all.at[m], clean_all.at[m], s_c.at[t], r_c.at[t], in_plane(t))

    @pl.loop(0, 15)
    def _(t):
        spread(t).start()

    @pl.loop(0, 15)
    def _(t):
        at = chunk_from(t)
        send(clean_all.at[at], clean_all.at[at], s_c.at[t], r_c.at[t], in_plane(t)).wait_recv()

    for low in range(2):
        for q in range(8):
            centered = (clean_all[low * 8 + q].astype(F32) - db_c[...]).astype(BF16).astype(F32)
            for j in range(T):
                cent[low, 4 * q : 4 * q + 4, 128 * j : 128 * j + 128] = centered[4 * j : 4 * j + 4, :]
        lhs[32 * low : 32 * low + 32, :] = cent[low].astype(BF16)

    loads[7].wait()
    for share in shared:
        share.wait_recv()
    pre_act = jnp.dot(lhs[...], enc[...], preferred_element_type=F32) + eb[...]
    lat[...] = jnp.maximum(pre_act, 0.0).astype(BF16)
    lat_src[...] = lat[:, 256:512]
    swap = send(lat_src, lat_land, s_l.at[0], r_l.at[0], other)

    cuts = ((0, 384), (384, 256), (640, 256))

    def e1(h, t):
        to_x, to_y = lax.rem(x + around(t // 4, 4), 4), lax.rem(y + around(lax.rem(t, 4), 4), 4)
        rows = pl.ds(pl.multiple_of(32 * lax.rem(to_y, 2) + 16 * (to_y // 2), 16), 16)
        cols = pl.ds(*cuts[h])
        return send(
            e_src.at[t // 4, rows, cols], land_e1.at[t, :, cols], s_e1.at[h, t], r_e1.at[h, t], plane_at(to_x, to_y)
        )

    loads[8].wait()
    for h, (low, count) in enumerate(cuts):
        for g in range(4):
            first_col = lax.rem(x + around(jnp.int32(g), 4), 4) * 896 + low
            cols = pl.ds(pl.multiple_of(first_col, 128), count)
            own = jnp.dot(lat[...], dec[:, cols], preferred_element_type=F32)
            if g == 3:
                e_own[:, low : low + count] = own
            e_src[g, :, low : low + count] = own.astype(BF16)

            @pl.loop(4 * g, min(4 * g + 4, 15))
            def _(t, h=h):
                e1(h, t).start()

    swap.start()

    def layer(h, stream):
        squares = jnp.zeros((32, 128), F32)
        for j in range(T):
            tile = stream[:, 128 * j : 128 * j + 128]
            squares += tile * tile
        scale = lax.rsqrt(jnp.sum(squares, axis=1, keepdims=True) / D + EPS)
        for g in range(7):
            cols = slice(512 * g, 512 * g + 512)
            lhs_f[h, :, cols] = (stream[:, cols] * scale * gpre_row[0:1, cols]).astype(BF16)
        gate_out = lax.dot_general(lhs_f[h], gate[...], (((1,), (1,)), ((), ())), preferred_element_type=F32)
        up_out = lax.dot_general(lhs_f[h], up[...], (((1,), (1,)), ((), ())), preferred_element_type=F32)
        act = (gelu(gate_out) * up_out).astype(BF16)
        for g in range(4):
            part = jnp.dot(act, d2[:, 896 * g : 896 * g + 896], preferred_element_type=F32)
            for half in range(2):
                piece = part[:, 448 * half : 448 * half + 448]
                f_own[h, 2 * g + half, :, 0:448] = piece
                f_src[h, 2 * g + half, :, 0:448] = piece.astype(BF16)

    for q in range(8):
        clean = clean_all[yl * 8 + q].astype(F32)
        for j in range(T):
            clean_u[4 * q : 4 * q + 4, 128 * j : 128 * j + 128] = clean[4 * j : 4 * j + 4, :]
    loads[9].wait()
    loads[10].wait()
    loads[11].wait()
    layer(0, clean_u)

    row = pl.multiple_of(32 * yl + 16 * yh, 16)

    def e2(h, t):
        cols = pl.ds(*cuts[h])
        return send(send_e2.at[:, cols], land_e2.at[t, :, cols], s_e2.at[h, t], r_e2.at[h, t], in_z(t))

    def e3(h, t, at):
        cols = pl.ds(*cuts[h])
        return send(recon_p.at[at, :, cols], recon_p.at[at, :, cols], s_e3.at[h, t], r_e3.at[h, t], in_k(t))

    def f1(h, q, t):
        rows = pl.ds(16 * q, 16)
        return send(
            f_src.at[h, k_at(t), rows, :], land_f1.at[h, t, rows, :], s_f1.at[h, q, t], r_f1.at[h, q, t], in_k(t)
        )

    def f2(h, q, t):
        rows = pl.ds(16 * q, 16)
        return send(
            send_f2.at[h, rows, :], land_f2.at[h, t, rows, :], s_f2.at[h, q, t], r_f2.at[h, q, t], in_z(t)
        )

    def f3(h, t):
        return send(send_f3.at[h], land_f3.at[h, t], s_f3.at[h, t], r_f3.at[h, t], in_k(t))

    def start_f1(h):
        for q in range(2):

            @pl.loop(0, 7)
            def _(t, q=q):
                f1(h, q, t).start()

    sums = []
    for h, (low, count) in enumerate(cuts):
        for t in range(15):
            e1(h, t).wait_recv()
        total = e_own[pl.ds(row, 16), low : low + count]
        for t in range(15):
            total += land_e1[t, :, low : low + count].astype(F32)
        send_e2[:, low : low + count] = total.astype(BF16)

        @pl.loop(0, 7)
        def _(t, h=h):
            e2(h, t).start()

        sums.append(total)

    start_f1(0)

    for h, (low, count) in enumerate(cuts):
        for t in range(7):
            e2(h, t).wait_recv()
        for t in range(7):
            sums[h] += land_e2[t, :, low : low + count].astype(F32)
        recon_p[k, :, low : low + count] = (sums[h] + db_row[x, 0:1, low : low + count]).astype(BF16)

        @pl.loop(0, 7)
        def _(t, h=h):
            e3(h, t, k).start()

    def sum_over_k(h):
        for q in range(2):
            rows = slice(16 * q, 16 * q + 16)
            for t in range(7):
                f1(h, q, t).wait_recv()
            total = f_own[h, k, rows, :]
            for t in range(7):
                total += land_f1[h, t, rows, :].astype(F32)
            f_sum[h, rows, :] = total
            send_f2[h, rows, :] = total.astype(BF16)

            @pl.loop(0, 7)
            def _(t, q=q):
                f2(h, q, t).start()

    diagonal = (
        lax.broadcasted_iota(jnp.int32, (32, 128), 0) == lax.broadcasted_iota(jnp.int32, (32, 128), 1)
    ).astype(F32)

    def sum_over_z(h):
        for q in range(2):
            for t in range(7):
                f2(h, q, t).wait_recv()
        total = f_sum[h]
        for t in range(7):
            total += land_f2[h, t].astype(F32)
        second[h, :, 0:512] = total
        squares = jnp.sum(total * total, axis=1, keepdims=True)
        flat = jnp.sum(squares * diagonal, axis=0, keepdims=True)
        send_f3[h] = jnp.broadcast_to(flat, (8, 128))

        @pl.loop(0, 7)
        def _(t):
            f3(h, t).start()

    def outputs(h, stream):
        for t in range(7):
            f3(h, t).wait_recv()
        flat = send_f3[h]
        for t in range(7):
            flat += land_f3[h, t]
        squares = jnp.sum(flat[0:1, :] * diagonal, axis=1, keepdims=True)
        gain = pick(gpost_row, 56 * s, 8)[0:1, :]
        return pick(stream, 56 * s, 32) + pick(second.at[h], 56 * z, 32) * lax.rsqrt(squares / D + EPS) * gain

    sum_over_k(0)

    for h in range(3):
        for t in range(7):
            e3(h, t, k_from(t)).wait_recv()
    for q in range(8):
        row, col = 16 * (q % 2), 896 * (q // 2)
        recon_u[row : row + 16, col : col + 896] = recon_p[q].astype(F32)
    layer(1, recon_u)

    start_f1(1)

    sum_over_z(0)
    sum_over_k(1)
    clean_out = outputs(0, clean_u)
    sum_over_z(1)
    delta_o[...] = outputs(1, recon_u) - clean_out

    swap.wait_recv()
    for low in range(2):
        rows = slice(32 * low, 32 * low + 32)
        lat_o[pl.ds(pl.multiple_of(64 * low + 32 * c, 32), 32), :] = lat[rows, 0:256]
        lat_o[pl.ds(pl.multiple_of(64 * low + 32 - 32 * c, 32), 32), :] = lat_land[rows, :]

    @pl.loop(0, 7)
    def _(t):
        for h in range(3):
            b1(h, t).wait_send()
            b2(h, t).wait_send()
            e2(h, t).wait_send()
            e3(h, t, k).wait_send()
        for h in range(2):
            f3(h, t).wait_send()
            for q in range(2):
                f1(h, q, t).wait_send()
                f2(h, q, t).wait_send()

    @pl.loop(0, 15)
    def _(t):
        spread(t).wait_send()
        for h in range(3):
            e1(h, t).wait_send()

    swap.wait_send()
    for share in shared:
        share.wait_send()


def on_device(
    hidden_in, resid, down_one, gain_one, enc_weight, enc_bias, dec_weight, dec_bias, gain_pre, gate_two, up_two,
    down_two, gain_post,
):
    tiles = (T, 128)
    args = (
        hidden_in, resid, down_one, gain_one.reshape(tiles), enc_weight, enc_bias.reshape(1, 256), dec_weight,
        dec_bias.reshape(tiles), gain_pre.reshape(tiles), gate_two.T, up_two.T, down_two,
        gain_post.reshape(tiles),
    )
    held = {4: (D, 512), 5: (1, 512), 6: (512, D)}
    dma = pltpu.SemaphoreType.DMA
    vmem = pltpu.VMEM
    latents, delta = pl.pallas_call(
        kernel,
        name="spliced",
        out_shape=(vmem((128, 256), BF16), vmem((32, 128), F32)),
        in_specs=[pl.BlockSpec(memory_space=pl.ANY)] * len(args),
        out_specs=[pl.BlockSpec(memory_space=pltpu.VMEM)] * 2,
        scratch_shapes=[vmem(held.get(i, a.shape), a.dtype) for i, a in enumerate(args)]
        + [
            vmem((8, 112, 128), F32),
            vmem((8, 112, 128), BF16),
            vmem((8, 112, 128), BF16),
            vmem((112, 128), BF16),
            vmem((8, 112, 128), BF16),
            vmem((8, 112, 128), F32),
            vmem((112, 128), F32),
            vmem((112, 128), F32),
            vmem((4, 8, 896), F32),
            vmem((8, D), F32),
            vmem((8, D + 128), F32),
            vmem((16, 112, 128), BF16),
            vmem((2, 32, D), F32),
            vmem((64, D), BF16),
            vmem((64, 512), BF16),
            vmem((64, 256), BF16),
            vmem((64, 256), BF16),
            vmem((4, 64, 896), BF16),
            vmem((64, 896), F32),
            vmem((16, 16, 896), BF16),
            vmem((16, 896), BF16),
            vmem((8, 16, 896), BF16),
            vmem((8, 16, 896), BF16),
            vmem((32, D + 128), F32),
            vmem((32, D + 128), F32),
            vmem((2, 32, D), BF16),
            vmem((2, 8, 32, 512), BF16),
            vmem((2, 8, 32, 512), F32),
            vmem((2, 8, 32, 512), BF16),
            vmem((2, 32, 512), F32),
            vmem((2, 32, 512), BF16),
            vmem((2, 8, 32, 512), BF16),
            vmem((2, 32, 640), F32),
            vmem((2, 8, 128), F32),
            vmem((2, 8, 8, 128), F32),
            dma((7,)), dma((12,)),
            dma((3, 7)), dma((3, 7)), dma((3, 7)), dma((3, 7)),
            dma((3,)), dma((3,)), dma((15,)), dma((15,)), dma((1,)), dma((1,)),
            dma((3, 15)), dma((3, 15)), dma((3, 7)), dma((3, 7)), dma((3, 7)), dma((3, 7)),
            dma((2, 2, 7)), dma((2, 2, 7)), dma((2, 2, 7)), dma((2, 2, 7)), dma((2, 7)), dma((2, 7)),
        ],
        compiler_params=pltpu.CompilerParams(
            collective_id=0, has_side_effects=True, vmem_limit_bytes=62 * 2**20
        ),
        cost_estimate=pl.CostEstimate(flops=10**9, bytes_accessed=12 * 10**6, transcendentals=10**5),
    )(*args)
    return latents, delta[:, :56]


def solution(mesh):
    in_specs = (
        P("rows", "shard"),
        P("rows", None),
        P("shard", None),
        P(),
        P(None, ("rows", "shard")),
        P(("rows", "shard")),
        P(("rows", "shard"), None),
        P(),
        P(),
        P(None, "shard"),
        P(None, "shard"),
        P("shard", None),
        P(),
    )
    out_specs = (P(None, ("rows", "shard")), P("rows", "shard"))
    return jax.shard_map(on_device, mesh=mesh, in_specs=in_specs, out_specs=out_specs, check_vma=False)
```

```python
import functools

import jax
import jax.numpy as jnp
from jax import lax
from jax.experimental import pallas as pl
from jax.experimental.pallas import tpu as pltpu
from jax.sharding import PartitionSpec as P

D = 3584
T = D // 128
MESH = pl.DeviceIdType.MESH
F32, BF16 = jnp.float32, jnp.bfloat16
EPS = 1e-06


def pick(ref, start, rows):
    tile, turn = start // 128, lax.rem(start, 128)
    lo = ref[0:rows, pl.ds(pl.multiple_of(tile * 128, 128), 128)]
    hi = ref[0:rows, pl.ds(pl.multiple_of(tile * 128 + 128, 128), 128)]
    shift = lax.rem(128 - turn, 128)
    lane = lax.broadcasted_iota(jnp.int32, (rows, 128), 1)
    return jnp.where(lane < 128 - turn, pltpu.roll(lo, shift, 1), pltpu.roll(hi, shift, 1))


def around(t, n):
    return (n // 2 + n + (1 - 2 * (t % 2)) * ((t + 1) // 2)) % n


def gelu(v):
    return 0.5 * v * (1.0 + jnp.tanh(0.7978845608028654 * (v + 0.044715 * (v * v * v))))


def kernel(
    hid_h, resid_h, d1_h, g1_h, enc_h, eb_h, dec_h, db_h, gpre_h, gate_h, up_h, d2_h, gpost_h,
    lat_o, delta_o,
    hid, resid, d1, g1, enc, eb, dec, db, gpre, gate, up, d2, gpost,
    parts, parts_b, land_b1, send_b2, land_b2, resid_c, g1_c, db_c, db_row, gpre_row, gpost_row,
    clean_all, cent, lhs, lat, lat_src, lat_land, e_src, e_own, land_e1, send_e2, land_e2, recon_p,
    clean_u, recon_u, lhs_f, f_src, f_own, land_f1, f_sum, send_f2, land_f2, second, send_f3, land_f3,
    d1_sem, load_sem, s_b1, r_b1, s_b2, r_b2, s_w, r_w, s_c, r_c, s_l, r_l, s_e1, r_e1, s_e2, r_e2, s_e3, r_e3,
    s_f1, r_f1, s_f2, r_f2, s_f3, r_f3,
):
    r = lax.axis_index("rows")
    s = lax.axis_index("shard")
    yl, c = r // 2, lax.rem(r, 2)
    k, z = s // 8, lax.rem(s, 8)
    x, yh = k // 2, lax.rem(k, 2)
    y, m = 2 * yh + yl, yl * 8 + k
    other = (yl * 2 + 1 - c, s)

    def k_at(t):
        return lax.rem(x + around(t // 2, 4), 4) * 2 + lax.rem(yh + 1 - t % 2, 2)

    def k_from(t):
        return lax.rem(x + 4 - around(t // 2, 4), 4) * 2 + lax.rem(yh + 1 - t % 2, 2)

    def in_k(t):
        return (r, k_at(t) * 8 + z)

    def in_z(t):
        return (r, k * 8 + lax.rem(z + around(t, 8), 8))

    def plane_at(to_x, to_y):
        return (lax.rem(to_y, 2) * 2 + c, (to_x * 2 + to_y // 2) * 8 + z)

    def in_plane(t):
        return plane_at(lax.rem(x + around(t // 4, 4), 4), lax.rem(y + around(t % 4, 4), 4))

    def chunk_from(t):
        from_x = lax.rem(x + 4 - around(t // 4, 4), 4)
        from_y = lax.rem(y + 4 - around(t % 4, 4), 4)
        return lax.rem(from_y, 2) * 8 + from_x * 2 + from_y // 2

    def send(src, dst, s_sem, r_sem, device):
        return pltpu.make_async_remote_copy(
            src_ref=src, dst_ref=dst, send_sem=s_sem, recv_sem=r_sem, device_id=device, device_id_type=MESH
        )

    def first_load(g):
        cols = pl.ds(512 * g, 512)
        return pltpu.make_async_copy(d1_h.at[:, cols], d1.at[:, cols], d1_sem.at[g])

    loads = [
        pltpu.make_async_copy(a, b, load_sem.at[i])
        for i, (a, b) in enumerate(
            (
                (hid_h, hid), (resid_h, resid), (g1_h, g1), (db_h, db), (gpre_h, gpre), (gpost_h, gpost),
                (eb_h, eb.at[:, pl.ds(0, 256)]), (enc_h, enc.at[:, pl.ds(0, 256)]), (dec_h, dec.at[pl.ds(0, 256), :]),
                (gate_h, gate), (up_h, up), (d2_h, d2),
            )
        )
    ]
    loads[0].start()
    for g in range(7):
        first_load(g).start()

    barrier = pltpu.get_barrier_semaphore()
    for t in range(15):
        pl.semaphore_signal(barrier, inc=1, device_id=in_plane(t), device_id_type=MESH)
    for t in range(7):
        pl.semaphore_signal(barrier, inc=1, device_id=in_z(t), device_id_type=MESH)

    pl.semaphore_signal(barrier, inc=1, device_id=other, device_id_type=MESH)

    thirds = ((0, 32), (32, 32), (64, 48))

    def b1(h, t):
        rows = pl.ds(*thirds[h])
        return send(
            parts_b.at[k_at(t), rows, :], land_b1.at[t, rows, :], s_b1.at[h, t], r_b1.at[h, t], in_k(t)
        )

    loads[0].wait()
    for g in range(7):
        first_load(g).wait()
        part = jnp.dot(hid[...], d1[:, 512 * g : 512 * g + 512], preferred_element_type=F32)
        for j in range(4):
            row = 4 * (4 * g + j)
            for piece in range(8):
                parts[piece, row : row + 4, :] = part[4 * piece : 4 * piece + 4, 128 * j : 128 * j + 128]
        if g in (1, 3, 6):
            h = (1, 3, 6).index(g)
            rows = slice(thirds[h][0], sum(thirds[h]))
            for piece in range(8):
                parts_b[piece, rows, :] = parts[piece, rows, :].astype(BF16)
            if h == 0:
                pl.semaphore_wait(barrier, 23)
            for t in range(7):
                b1(h, t).start()

    for load in loads[1:]:
        load.start()
    shared = [
        send(a, b, s_w.at[i], r_w.at[i], other)
        for i, (a, b) in enumerate(
            (
                (eb_h, eb.at[:, pl.ds(256, 256)]),
                (enc_h, enc.at[:, pl.ds(256, 256)]),
                (dec_h, dec.at[pl.ds(256, 256), :]),
            )
        )
    ]
    for share in shared:
        share.start()

    for i in range(1, 7):
        loads[i].wait()
    for j in range(T):
        tile = slice(128 * j, 128 * j + 128)
        old = resid[:, tile].astype(F32)
        for piece in range(8):
            resid_c[piece, 4 * j : 4 * j + 4, :] = old[4 * piece : 4 * piece + 4, :]
        g1_c[4 * j : 4 * j + 4, :] = jnp.broadcast_to(g1[j : j + 1, :], (4, 128))
        db_c[4 * j : 4 * j + 4, :] = jnp.broadcast_to(db[j : j + 1, :], (4, 128))
        gpre_row[:, tile] = jnp.broadcast_to(gpre[j : j + 1, :], (8, 128))
        gpost_row[:, tile] = jnp.broadcast_to(gpost[j : j + 1, :], (8, 128))
        db_row[j // 7, :, 128 * (j % 7) : 128 * (j % 7) + 128] = jnp.broadcast_to(db[j : j + 1, :], (8, 128))
    gpost_row[:, D:] = jnp.zeros((8, 128), F32)
    clean_u[:, D:] = jnp.zeros((32, 128), F32)
    recon_u[:, D:] = jnp.zeros((32, 128), F32)
    second[:, :, 448:] = jnp.zeros((2, 32, 192), F32)

    def b2(h, t):
        rows = pl.ds(*thirds[h])
        return send(send_b2.at[rows, :], land_b2.at[t, rows, :], s_b2.at[h, t], r_b2.at[h, t], in_z(t))

    sums = []
    for h, (low, count) in enumerate(thirds):
        for t in range(7):
            b1(h, t).wait_recv()
        total = parts[k, low : low + count, :]
        for t in range(7):
            total += land_b1[t, low : low + count, :].astype(F32)
        send_b2[low : low + count, :] = total.astype(BF16)
        for t in range(7):
            b2(h, t).start()

        sums.append(total)

    for h, (low, count) in enumerate(thirds):
        for t in range(7):
            b2(h, t).wait_recv()
        for t in range(7):
            sums[h] += land_b2[t, low : low + count, :].astype(F32)
    total = jnp.concatenate(sums, axis=0)
    squares = total[0:8] * total[0:8]
    for i in range(1, 14):
        squares += total[8 * i : 8 * i + 8] * total[8 * i : 8 * i + 8]
    squares += pltpu.roll(squares, 4, 0)
    scale = lax.rsqrt(jnp.sum(squares, axis=1, keepdims=True) / D + EPS)
    scale = jnp.concatenate([jnp.broadcast_to(scale, (8, 128))] * 14, axis=0)
    clean_all[m] = (resid_c[k] + total * scale * g1_c[...]).astype(BF16)

    def spread(t):
        return send(clean_all.at[m], clean_all.at[m], s_c.at[t], r_c.at[t], in_plane(t))

    for t in range(15):
        spread(t).start()

    for t in range(15):
        at = chunk_from(t)
        send(clean_all.at[at], clean_all.at[at], s_c.at[t], r_c.at[t], in_plane(t)).wait_recv()

    for low in range(2):
        for q in range(8):
            centered = (clean_all[low * 8 + q].astype(F32) - db_c[...]).astype(BF16).astype(F32)
            for j in range(T):
                cent[low, 4 * q : 4 * q + 4, 128 * j : 128 * j + 128] = centered[4 * j : 4 * j + 4, :]
        lhs[32 * low : 32 * low + 32, :] = cent[low].astype(BF16)

    loads[7].wait()
    for share in shared:
        share.wait_recv()
    pre_act = jnp.dot(lhs[...], enc[...], preferred_element_type=F32) + eb[...]
    lat[...] = jnp.maximum(pre_act, 0.0).astype(BF16)
    lat_src[...] = lat[:, 256:512]
    swap = send(lat_src, lat_land, s_l.at[0], r_l.at[0], other)

    cuts = ((0, 384), (384, 256), (640, 256))

    def e1(h, t):
        to_x, to_y = lax.rem(x + around(t // 4, 4), 4), lax.rem(y + around(t % 4, 4), 4)
        rows = pl.ds(pl.multiple_of(32 * lax.rem(to_y, 2) + 16 * (to_y // 2), 16), 16)
        cols = pl.ds(*cuts[h])
        return send(
            e_src.at[t // 4, rows, cols], land_e1.at[t, :, cols], s_e1.at[h, t], r_e1.at[h, t], plane_at(to_x, to_y)
        )

    loads[8].wait()
    for h, (low, count) in enumerate(cuts):
        for g in range(4):
            first_col = lax.rem(x + around(g, 4), 4) * 896 + low
            cols = pl.ds(pl.multiple_of(first_col, 128), count)
            own = jnp.dot(lat[...], dec[:, cols], preferred_element_type=F32)
            if g == 3:
                e_own[:, low : low + count] = own
            e_src[g, :, low : low + count] = own.astype(BF16)
            for t in range(4 * g, min(4 * g + 4, 15)):
                e1(h, t).start()

    swap.start()

    def layer(h, stream):
        squares = jnp.zeros((32, 128), F32)
        for j in range(T):
            tile = stream[:, 128 * j : 128 * j + 128]
            squares += tile * tile
        scale = lax.rsqrt(jnp.sum(squares, axis=1, keepdims=True) / D + EPS)
        for g in range(7):
            cols = slice(512 * g, 512 * g + 512)
            lhs_f[h, :, cols] = (stream[:, cols] * scale * gpre_row[0:1, cols]).astype(BF16)
        gate_out = lax.dot_general(lhs_f[h], gate[...], (((1,), (1,)), ((), ())), preferred_element_type=F32)
        up_out = lax.dot_general(lhs_f[h], up[...], (((1,), (1,)), ((), ())), preferred_element_type=F32)
        act = (gelu(gate_out) * up_out).astype(BF16)
        for g in range(4):
            part = jnp.dot(act, d2[:, 896 * g : 896 * g + 896], preferred_element_type=F32)
            for half in range(2):
                piece = part[:, 448 * half : 448 * half + 448]
                top, low = piece[0:16, :], piece[16:32, :]
                ends = jnp.concatenate([top[:, 384:448], low[:, 384:448]], axis=1)
                packed = jnp.concatenate([top[:, 0:384], low[:, 0:384], ends], axis=1)
                f_own[h, 2 * g + half] = packed
                f_src[h, 2 * g + half] = packed.astype(BF16)

    for q in range(8):
        clean = clean_all[yl * 8 + q].astype(F32)
        for j in range(T):
            clean_u[4 * q : 4 * q + 4, 128 * j : 128 * j + 128] = clean[4 * j : 4 * j + 4, :]
    loads[9].wait()
    loads[10].wait()
    loads[11].wait()
    layer(0, clean_u)

    row = pl.multiple_of(32 * yl + 16 * yh, 16)

    def e2(h, t):
        cols = pl.ds(*cuts[h])
        return send(send_e2.at[:, cols], land_e2.at[t, :, cols], s_e2.at[h, t], r_e2.at[h, t], in_z(t))

    def e3(h, t, at):
        cols = pl.ds(*cuts[h])
        return send(recon_p.at[at, :, cols], recon_p.at[at, :, cols], s_e3.at[h, t], r_e3.at[h, t], in_k(t))

    def f1(h, q, t):
        cols = pl.ds(*cuts[q])
        return send(
            f_src.at[h, k_at(t), :, cols], land_f1.at[h, t, :, cols], s_f1.at[h, q, t], r_f1.at[h, q, t], in_k(t)
        )

    def f2(h, q, t):
        cols = pl.ds(*cuts[q])
        return send(
            send_f2.at[h, :, cols], land_f2.at[h, t, :, cols], s_f2.at[h, q, t], r_f2.at[h, q, t], in_z(t)
        )

    def f3(h, t):
        return send(send_f3.at[h], land_f3.at[h, t], s_f3.at[h, t], r_f3.at[h, t], in_k(t))

    def start_f1(h):
        for q in range(3):
            for t in range(7):
                f1(h, q, t).start()

    sums = []
    for h, (low, count) in enumerate(cuts):
        for t in range(15):
            e1(h, t).wait_recv()
        total = e_own[pl.ds(row, 16), low : low + count]
        for t in range(15):
            total += land_e1[t, :, low : low + count].astype(F32)
        send_e2[:, low : low + count] = total.astype(BF16)
        for t in range(7):
            e2(h, t).start()

        sums.append(total)

    start_f1(0)

    for h, (low, count) in enumerate(cuts):
        for t in range(7):
            e2(h, t).wait_recv()
        for t in range(7):
            sums[h] += land_e2[t, :, low : low + count].astype(F32)
        recon_p[k, :, low : low + count] = (sums[h] + db_row[x, 0:1, low : low + count]).astype(BF16)
        for t in range(7):
            e3(h, t, k).start()

    def sum_over_k(h):
        for q, (low, count) in enumerate(cuts):
            cols = slice(low, low + count)
            for t in range(7):
                f1(h, q, t).wait_recv()
            total = f_own[h, k, :, cols]
            for t in range(7):
                total += land_f1[h, t, :, cols].astype(F32)
            f_sum[h, :, cols] = total
            send_f2[h, :, cols] = total.astype(BF16)
            for t in range(7):
                f2(h, q, t).start()

    diagonal = (
        lax.broadcasted_iota(jnp.int32, (32, 128), 0) == lax.broadcasted_iota(jnp.int32, (32, 128), 1)
    ).astype(F32)

    def sum_over_z(h):
        for q, (low, count) in enumerate(cuts):
            cols = slice(low, low + count)
            for t in range(7):
                f2(h, q, t).wait_recv()
            total = f_sum[h, :, cols]
            for t in range(7):
                total += land_f2[h, t, :, cols].astype(F32)
            f_sum[h, :, cols] = total
        second[h, 0:16, 0:384] = f_sum[h, :, 0:384]
        second[h, 16:32, 0:384] = f_sum[h, :, 384:768]
        second[h, 0:16, 384:448] = f_sum[h, :, 768:832]
        second[h, 16:32, 384:448] = f_sum[h, :, 832:896]
        total = second[h, :, 0:512]
        squares = jnp.sum(total * total, axis=1, keepdims=True)
        flat = jnp.sum(squares * diagonal, axis=0, keepdims=True)
        send_f3[h] = jnp.broadcast_to(flat, (8, 128))
        for t in range(7):
            f3(h, t).start()

    def outputs(h, stream):
        for t in range(7):
            f3(h, t).wait_recv()
        flat = send_f3[h]
        for t in range(7):
            flat += land_f3[h, t]
        squares = jnp.sum(flat[0:1, :] * diagonal, axis=1, keepdims=True)
        gain = pick(gpost_row, 56 * s, 8)[0:1, :]
        return pick(stream, 56 * s, 32) + pick(second.at[h], 56 * z, 32) * lax.rsqrt(squares / D + EPS) * gain

    sum_over_k(0)

    for h in range(3):
        for t in range(7):
            e3(h, t, k_from(t)).wait_recv()
    for q in range(8):
        row, col = 16 * (q % 2), 896 * (q // 2)
        recon_u[row : row + 16, col : col + 896] = recon_p[q].astype(F32)
    layer(1, recon_u)

    start_f1(1)

    sum_over_z(0)
    sum_over_k(1)
    clean_out = outputs(0, clean_u)
    sum_over_z(1)
    delta_o[...] = outputs(1, recon_u) - clean_out

    swap.wait_recv()
    for low in range(2):
        rows = slice(32 * low, 32 * low + 32)
        lat_o[pl.ds(pl.multiple_of(64 * low + 32 * c, 32), 32), :] = lat[rows, 0:256]
        lat_o[pl.ds(pl.multiple_of(64 * low + 32 - 32 * c, 32), 32), :] = lat_land[rows, :]

    for t in range(7):
        for h in range(3):
            b1(h, t).wait_send()
            b2(h, t).wait_send()
            e2(h, t).wait_send()
            e3(h, t, k).wait_send()
        for h in range(2):
            f3(h, t).wait_send()
            for q in range(3):
                f1(h, q, t).wait_send()
                f2(h, q, t).wait_send()
    for t in range(15):
        spread(t).wait_send()
        for h in range(3):
            e1(h, t).wait_send()

    swap.wait_send()
    for share in shared:
        share.wait_send()


def on_device(
    hidden_in, resid, down_one, gain_one, enc_weight, enc_bias, dec_weight, dec_bias, gain_pre, gate_two, up_two,
    down_two, gain_post,
):
    tiles = (T, 128)
    args = (
        hidden_in, resid, down_one, gain_one.reshape(tiles), enc_weight, enc_bias.reshape(1, 256), dec_weight,
        dec_bias.reshape(tiles), gain_pre.reshape(tiles), gate_two.T, up_two.T, down_two,
        gain_post.reshape(tiles),
    )
    held = {4: (D, 512), 5: (1, 512), 6: (512, D)}
    dma = pltpu.SemaphoreType.DMA
    vmem = pltpu.VMEM
    latents, delta = pl.pallas_call(
        kernel,
        name="spliced",
        out_shape=(vmem((128, 256), BF16), vmem((32, 128), F32)),
        in_specs=[pl.BlockSpec(memory_space=pl.ANY)] * len(args),
        out_specs=[pl.BlockSpec(memory_space=pltpu.VMEM)] * 2,
        scratch_shapes=[vmem(held.get(i, a.shape), a.dtype) for i, a in enumerate(args)]
        + [
            vmem((8, 112, 128), F32),
            vmem((8, 112, 128), BF16),
            vmem((8, 112, 128), BF16),
            vmem((112, 128), BF16),
            vmem((8, 112, 128), BF16),
            vmem((8, 112, 128), F32),
            vmem((112, 128), F32),
            vmem((112, 128), F32),
            vmem((4, 8, 896), F32),
            vmem((8, D), F32),
            vmem((8, D + 128), F32),
            vmem((16, 112, 128), BF16),
            vmem((2, 32, D), F32),
            vmem((64, D), BF16),
            vmem((64, 512), BF16),
            vmem((64, 256), BF16),
            vmem((64, 256), BF16),
            vmem((4, 64, 896), BF16),
            vmem((64, 896), F32),
            vmem((16, 16, 896), BF16),
            vmem((16, 896), BF16),
            vmem((8, 16, 896), BF16),
            vmem((8, 16, 896), BF16),
            vmem((32, D + 128), F32),
            vmem((32, D + 128), F32),
            vmem((2, 32, D), BF16),
            vmem((2, 8, 16, 896), BF16),
            vmem((2, 8, 16, 896), F32),
            vmem((2, 8, 16, 896), BF16),
            vmem((2, 16, 896), F32),
            vmem((2, 16, 896), BF16),
            vmem((2, 8, 16, 896), BF16),
            vmem((2, 32, 640), F32),
            vmem((2, 8, 128), F32),
            vmem((2, 8, 8, 128), F32),
            dma((7,)), dma((12,)),
            dma((3, 7)), dma((3, 7)), dma((3, 7)), dma((3, 7)),
            dma((3,)), dma((3,)), dma((15,)), dma((15,)), dma((1,)), dma((1,)),
            dma((3, 15)), dma((3, 15)), dma((3, 7)), dma((3, 7)), dma((3, 7)), dma((3, 7)),
            dma((2, 3, 7)), dma((2, 3, 7)), dma((2, 3, 7)), dma((2, 3, 7)), dma((2, 7)), dma((2, 7)),
        ],
        compiler_params=pltpu.CompilerParams(
            collective_id=0, has_side_effects=True, vmem_limit_bytes=62 * 2**20
        ),
        cost_estimate=pl.CostEstimate(flops=10**9, bytes_accessed=12 * 10**6, transcendentals=10**5),
    )(*args)
    return latents, delta[:, :56]


def solution(mesh):
    in_specs = (
        P("rows", "shard"),
        P("rows", None),
        P("shard", None),
        P(),
        P(None, ("rows", "shard")),
        P(("rows", "shard")),
        P(("rows", "shard"), None),
        P(),
        P(),
        P(None, "shard"),
        P(None, "shard"),
        P("shard", None),
        P(),
    )
    out_specs = (P(None, ("rows", "shard")), P("rows", "shard"))
    return jax.shard_map(on_device, mesh=mesh, in_specs=in_specs, out_specs=out_specs, check_vma=False)
```

```python
import functools

import jax
import jax.numpy as jnp
from jax import lax
from jax.experimental import pallas as pl
from jax.experimental.pallas import tpu as pltpu
from jax.sharding import PartitionSpec as P

D = 3584
T = D // 128
MESH = pl.DeviceIdType.MESH
F32, BF16 = jnp.float32, jnp.bfloat16
EPS = 1e-06


def pick(ref, start, rows):
    tile, turn = start // 128, lax.rem(start, 128)
    lo = ref[0:rows, pl.ds(pl.multiple_of(tile * 128, 128), 128)]
    hi = ref[0:rows, pl.ds(pl.multiple_of(tile * 128 + 128, 128), 128)]
    shift = lax.rem(128 - turn, 128)
    lane = lax.broadcasted_iota(jnp.int32, (rows, 128), 1)
    return jnp.where(lane < 128 - turn, pltpu.roll(lo, shift, 1), pltpu.roll(hi, shift, 1))


def around(t, n):
    return (n // 2 + n + (1 - 2 * (t % 2)) * ((t + 1) // 2)) % n


def gelu(v):
    return 0.5 * v * (1.0 + jnp.tanh(0.7978845608028654 * (v + 0.044715 * (v * v * v))))


def kernel(
    hid_h, resid_h, d1_h, g1_h, enc_h, eb_h, dec_h, db_h, gpre_h, gate_h, up_h, d2_h, gpost_h,
    lat_o, delta_o,
    hid, resid, d1, g1, enc, eb, dec, db, gpre, gate, up, d2, gpost,
    parts, parts_b, land_b1, send_b2, land_b2, resid_c, g1_c, db_c, db_row, gpre_row, gpost_row,
    clean_all, cent, lhs, lat, lat_src, lat_land, e_src, e_own, land_e1, send_e2, land_e2, recon_p,
    clean_u, recon_u, lhs_f, f_src, f_own, land_f1, f_sum, send_f2, land_f2, second, send_f3, land_f3,
    d1_sem, load_sem, s_b1, r_b1, s_b2, r_b2, s_w, r_w, s_c, r_c, s_l, r_l, s_e1, r_e1, s_e2, r_e2, s_e3, r_e3,
    s_f1, r_f1, s_f2, r_f2, s_f3, r_f3,
):
    r = lax.axis_index("rows")
    s = lax.axis_index("shard")
    yl, c = r // 2, lax.rem(r, 2)
    k, z = s // 8, lax.rem(s, 8)
    x, yh = k // 2, lax.rem(k, 2)
    y, m = 2 * yh + yl, yl * 8 + k
    other = (yl * 2 + 1 - c, s)

    def k_at(t):
        return lax.rem(x + around(t // 2, 4), 4) * 2 + lax.rem(yh + 1 - t % 2, 2)

    def k_from(t):
        return lax.rem(x + 4 - around(t // 2, 4), 4) * 2 + lax.rem(yh + 1 - t % 2, 2)

    def in_k(t):
        return (r, k_at(t) * 8 + z)

    def in_z(t):
        return (r, k * 8 + lax.rem(z + around(t, 8), 8))

    def plane_at(to_x, to_y):
        return (lax.rem(to_y, 2) * 2 + c, (to_x * 2 + to_y // 2) * 8 + z)

    def in_plane(t):
        return plane_at(lax.rem(x + around(t // 4, 4), 4), lax.rem(y + around(t % 4, 4), 4))

    def chunk_from(t):
        from_x = lax.rem(x + 4 - around(t // 4, 4), 4)
        from_y = lax.rem(y + 4 - around(t % 4, 4), 4)
        return lax.rem(from_y, 2) * 8 + from_x * 2 + from_y // 2

    def send(src, dst, s_sem, r_sem, device):
        return pltpu.make_async_remote_copy(
            src_ref=src, dst_ref=dst, send_sem=s_sem, recv_sem=r_sem, device_id=device, device_id_type=MESH
        )

    def first_load(g):
        cols = pl.ds(512 * g, 512)
        return pltpu.make_async_copy(d1_h.at[:, cols], d1.at[:, cols], d1_sem.at[g])

    loads = [
        pltpu.make_async_copy(a, b, load_sem.at[i])
        for i, (a, b) in enumerate(
            (
                (hid_h, hid), (resid_h, resid), (g1_h, g1), (db_h, db), (gpre_h, gpre), (gpost_h, gpost),
                (eb_h, eb.at[:, pl.ds(0, 256)]), (enc_h, enc.at[:, pl.ds(0, 256)]), (dec_h, dec.at[pl.ds(0, 256), :]),
                (gate_h, gate), (up_h, up), (d2_h, d2),
            )
        )
    ]
    loads[0].start()
    for g in range(7):
        first_load(g).start()

    barrier = pltpu.get_barrier_semaphore()
    for t in range(15):
        pl.semaphore_signal(barrier, inc=1, device_id=in_plane(t), device_id_type=MESH)
    for t in range(7):
        pl.semaphore_signal(barrier, inc=1, device_id=in_z(t), device_id_type=MESH)

    pl.semaphore_signal(barrier, inc=1, device_id=other, device_id_type=MESH)

    thirds = ((0, 32), (32, 32), (64, 48))

    def b1(h, t):
        rows = pl.ds(*thirds[h])
        return send(
            parts_b.at[k_at(t), rows, :], land_b1.at[t, rows, :], s_b1.at[h, t], r_b1.at[h, t], in_k(t)
        )

    loads[0].wait()
    for g in range(7):
        first_load(g).wait()
        part = jnp.dot(hid[...], d1[:, 512 * g : 512 * g + 512], preferred_element_type=F32)
        for j in range(4):
            row = 4 * (4 * g + j)
            for piece in range(8):
                parts[piece, row : row + 4, :] = part[4 * piece : 4 * piece + 4, 128 * j : 128 * j + 128]
        if g in (1, 3, 6):
            h = (1, 3, 6).index(g)
            rows = slice(thirds[h][0], sum(thirds[h]))
            for piece in range(8):
                parts_b[piece, rows, :] = parts[piece, rows, :].astype(BF16)
            if h == 0:
                pl.semaphore_wait(barrier, 23)
            for t in range(7):
                b1(h, t).start()

    for load in loads[1:]:
        load.start()
    shared = [
        send(a, b, s_w.at[i], r_w.at[i], other)
        for i, (a, b) in enumerate(
            (
                (eb_h, eb.at[:, pl.ds(256, 256)]),
                (enc_h, enc.at[:, pl.ds(256, 256)]),
                (dec_h, dec.at[pl.ds(256, 256), :]),
            )
        )
    ]
    for share in shared:
        share.start()

    for i in range(1, 7):
        loads[i].wait()
    for j in range(T):
        tile = slice(128 * j, 128 * j + 128)
        old = resid[:, tile].astype(F32)
        for piece in range(8):
            resid_c[piece, 4 * j : 4 * j + 4, :] = old[4 * piece : 4 * piece + 4, :]
        g1_c[4 * j : 4 * j + 4, :] = jnp.broadcast_to(g1[j : j + 1, :], (4, 128))
        db_c[4 * j : 4 * j + 4, :] = jnp.broadcast_to(db[j : j + 1, :], (4, 128))
        gpre_row[:, tile] = jnp.broadcast_to(gpre[j : j + 1, :], (8, 128))
        gpost_row[:, tile] = jnp.broadcast_to(gpost[j : j + 1, :], (8, 128))
        db_row[j // 7, :, 128 * (j % 7) : 128 * (j % 7) + 128] = jnp.broadcast_to(db[j : j + 1, :], (8, 128))
    gpost_row[:, D:] = jnp.zeros((8, 128), F32)
    clean_u[:, D:] = jnp.zeros((32, 128), F32)
    recon_u[:, D:] = jnp.zeros((32, 128), F32)
    second[:, :, 448:] = jnp.zeros((2, 32, 192), F32)

    def b2(h, t):
        rows = pl.ds(*thirds[h])
        return send(send_b2.at[rows, :], land_b2.at[t, rows, :], s_b2.at[h, t], r_b2.at[h, t], in_z(t))

    sums = []
    for h, (low, count) in enumerate(thirds):
        for t in range(7):
            b1(h, t).wait_recv()
        total = parts[k, low : low + count, :]
        for t in range(7):
            total += land_b1[t, low : low + count, :].astype(F32)
        send_b2[low : low + count, :] = total.astype(BF16)
        for t in range(7):
            b2(h, t).start()

        sums.append(total)

    for h, (low, count) in enumerate(thirds):
        for t in range(7):
            b2(h, t).wait_recv()
        for t in range(7):
            sums[h] += land_b2[t, low : low + count, :].astype(F32)
    total = jnp.concatenate(sums, axis=0)
    squares = total[0:8] * total[0:8]
    for i in range(1, 14):
        squares += total[8 * i : 8 * i + 8] * total[8 * i : 8 * i + 8]
    squares += pltpu.roll(squares, 4, 0)
    scale = lax.rsqrt(jnp.sum(squares, axis=1, keepdims=True) / D + EPS)
    scale = jnp.concatenate([jnp.broadcast_to(scale, (8, 128))] * 14, axis=0)
    clean_all[m] = (resid_c[k] + total * scale * g1_c[...]).astype(BF16)

    def spread(t):
        return send(clean_all.at[m], clean_all.at[m], s_c.at[t], r_c.at[t], in_plane(t))

    for t in range(15):
        spread(t).start()

    for t in range(15):
        at = chunk_from(t)
        send(clean_all.at[at], clean_all.at[at], s_c.at[t], r_c.at[t], in_plane(t)).wait_recv()

    for low in range(2):
        for q in range(8):
            centered = (clean_all[low * 8 + q].astype(F32) - db_c[...]).astype(BF16).astype(F32)
            for j in range(T):
                cent[low, 4 * q : 4 * q + 4, 128 * j : 128 * j + 128] = centered[4 * j : 4 * j + 4, :]
        lhs[32 * low : 32 * low + 32, :] = cent[low].astype(BF16)

    loads[7].wait()
    for share in shared:
        share.wait_recv()
    pre_act = jnp.dot(lhs[...], enc[...], preferred_element_type=F32) + eb[...]
    lat[...] = jnp.maximum(pre_act, 0.0).astype(BF16)
    lat_src[...] = lat[:, 256:512]
    swap = send(lat_src, lat_land, s_l.at[0], r_l.at[0], other)

    cuts = ((0, 384), (384, 256), (640, 256))

    def e1(h, t):
        to_x, to_y = lax.rem(x + around(t // 4, 4), 4), lax.rem(y + around(t % 4, 4), 4)
        rows = pl.ds(pl.multiple_of(32 * lax.rem(to_y, 2) + 16 * (to_y // 2), 16), 16)
        cols = pl.ds(*cuts[h])
        return send(
            e_src.at[t // 4, rows, cols], land_e1.at[t, :, cols], s_e1.at[h, t], r_e1.at[h, t], plane_at(to_x, to_y)
        )

    loads[8].wait()
    for h, (low, count) in enumerate(cuts):
        for g in range(4):
            first_col = lax.rem(x + around(g, 4), 4) * 896 + low
            cols = pl.ds(pl.multiple_of(first_col, 128), count)
            own = jnp.dot(lat[...], dec[:, cols], preferred_element_type=F32)
            if g == 3:
                e_own[:, low : low + count] = own
            e_src[g, :, low : low + count] = own.astype(BF16)
            for t in range(4 * g, min(4 * g + 4, 15)):
                e1(h, t).start()

    swap.start()

    def layer(h, stream):
        squares = jnp.zeros((32, 128), F32)
        for j in range(T):
            tile = stream[:, 128 * j : 128 * j + 128]
            squares += tile * tile
        scale = lax.rsqrt(jnp.sum(squares, axis=1, keepdims=True) / D + EPS)
        for g in range(7):
            cols = slice(512 * g, 512 * g + 512)
            lhs_f[h, :, cols] = (stream[:, cols] * scale * gpre_row[0:1, cols]).astype(BF16)
        gate_out = lax.dot_general(lhs_f[h], gate[...], (((1,), (1,)), ((), ())), preferred_element_type=F32)
        up_out = lax.dot_general(lhs_f[h], up[...], (((1,), (1,)), ((), ())), preferred_element_type=F32)
        act = (gelu(gate_out) * up_out).astype(BF16)
        for g in range(4):
            part = jnp.dot(act, d2[:, 896 * g : 896 * g + 896], preferred_element_type=F32)
            for half in range(2):
                piece = part[:, 448 * half : 448 * half + 448]
                top, low = piece[0:16, :], piece[16:32, :]
                ends = jnp.concatenate([top[:, 384:448], low[:, 384:448]], axis=1)
                packed = jnp.concatenate([top[:, 0:384], low[:, 0:384], ends], axis=1)
                f_own[h, 2 * g + half] = packed
                f_src[h, 2 * g + half] = packed.astype(BF16)

    for q in range(8):
        clean = clean_all[yl * 8 + q].astype(F32)
        for j in range(T):
            clean_u[4 * q : 4 * q + 4, 128 * j : 128 * j + 128] = clean[4 * j : 4 * j + 4, :]
    loads[9].wait()
    loads[10].wait()
    loads[11].wait()
    layer(0, clean_u)

    row = pl.multiple_of(32 * yl + 16 * yh, 16)

    def e2(h, t):
        cols = pl.ds(*cuts[h])
        return send(send_e2.at[:, cols], land_e2.at[t, :, cols], s_e2.at[h, t], r_e2.at[h, t], in_z(t))

    def e3(h, t, at):
        cols = pl.ds(*cuts[h])
        return send(recon_p.at[at, :, cols], recon_p.at[at, :, cols], s_e3.at[h, t], r_e3.at[h, t], in_k(t))

    def f1(h, q, t):
        cols = pl.ds(*cuts[q])
        return send(
            f_src.at[h, k_at(t), :, cols], land_f1.at[h, t, :, cols], s_f1.at[h, q, t], r_f1.at[h, q, t], in_k(t)
        )

    def f2(h, q, t):
        cols = pl.ds(*cuts[q])
        return send(
            send_f2.at[h, :, cols], land_f2.at[h, t, :, cols], s_f2.at[h, q, t], r_f2.at[h, q, t], in_z(t)
        )

    def f3(h, t):
        return send(send_f3.at[h], land_f3.at[h, t], s_f3.at[h, t], r_f3.at[h, t], in_k(t))

    def start_f1(h):
        for q in range(3):
            for t in range(7):
                f1(h, q, t).start()

    sums = []
    for h, (low, count) in enumerate(cuts):
        for t in range(15):
            e1(h, t).wait_recv()
        total = e_own[pl.ds(row, 16), low : low + count]
        for t in range(15):
            total += land_e1[t, :, low : low + count].astype(F32)
        send_e2[:, low : low + count] = total.astype(BF16)
        for t in range(7):
            e2(h, t).start()

        sums.append(total)

    start_f1(0)

    for h, (low, count) in enumerate(cuts):
        for t in range(7):
            e2(h, t).wait_recv()
        for t in range(7):
            sums[h] += land_e2[t, :, low : low + count].astype(F32)
        recon_p[k, :, low : low + count] = (sums[h] + db_row[x, 0:1, low : low + count]).astype(BF16)
        for t in range(7):
            e3(h, t, k).start()

    def sum_over_k(h):
        for q, (low, count) in enumerate(cuts):
            cols = slice(low, low + count)
            for t in range(7):
                f1(h, q, t).wait_recv()
            total = f_own[h, k, :, cols]
            for t in range(7):
                total += land_f1[h, t, :, cols].astype(F32)
            f_sum[h, :, cols] = total
            send_f2[h, :, cols] = total.astype(BF16)
            for t in range(7):
                f2(h, q, t).start()

    diagonal = (
        lax.broadcasted_iota(jnp.int32, (32, 128), 0) == lax.broadcasted_iota(jnp.int32, (32, 128), 1)
    ).astype(F32)

    def sum_over_z(h):
        for q, (low, count) in enumerate(cuts):
            cols = slice(low, low + count)
            for t in range(7):
                f2(h, q, t).wait_recv()
            total = f_sum[h, :, cols]
            for t in range(7):
                total += land_f2[h, t, :, cols].astype(F32)
            f_sum[h, :, cols] = total
        second[h, 0:16, 0:384] = f_sum[h, :, 0:384]
        second[h, 16:32, 0:384] = f_sum[h, :, 384:768]
        second[h, 0:16, 384:448] = f_sum[h, :, 768:832]
        second[h, 16:32, 384:448] = f_sum[h, :, 832:896]
        total = second[h, :, 0:512]
        squares = jnp.sum(total * total, axis=1, keepdims=True)
        flat = jnp.sum(squares * diagonal, axis=0, keepdims=True)
        send_f3[h] = jnp.broadcast_to(flat, (8, 128))
        for t in range(7):
            f3(h, t).start()

    def outputs(h, stream):
        for t in range(7):
            f3(h, t).wait_recv()
        flat = send_f3[h]
        for t in range(7):
            flat += land_f3[h, t]
        squares = jnp.sum(flat[0:1, :] * diagonal, axis=1, keepdims=True)
        gain = pick(gpost_row, 56 * s, 8)[0:1, :]
        return pick(stream, 56 * s, 32) + pick(second.at[h], 56 * z, 32) * lax.rsqrt(squares / D + EPS) * gain

    sum_over_k(0)

    for h in range(3):
        for t in range(7):
            e3(h, t, k_from(t)).wait_recv()
    for q in range(8):
        row, col = 16 * (q % 2), 896 * (q // 2)
        recon_u[row : row + 16, col : col + 896] = recon_p[q].astype(F32)
    layer(1, recon_u)

    start_f1(1)

    sum_over_z(0)
    sum_over_k(1)
    clean_out = outputs(0, clean_u)
    sum_over_z(1)
    swap.wait_recv()
    for low in range(2):
        rows = slice(32 * low, 32 * low + 32)
        lat_o[pl.ds(pl.multiple_of(64 * low + 32 * c, 32), 32), :] = lat[rows, 0:256]
        lat_o[pl.ds(pl.multiple_of(64 * low + 32 - 32 * c, 32), 32), :] = lat_land[rows, :]

    for t in range(7):
        for h in range(3):
            b1(h, t).wait_send()
            b2(h, t).wait_send()
            e2(h, t).wait_send()
            e3(h, t, k).wait_send()
        f3(0, t).wait_send()
        for h in range(2):
            for q in range(3):
                f1(h, q, t).wait_send()
                f2(h, q, t).wait_send()
    for t in range(15):
        spread(t).wait_send()
        for h in range(3):
            e1(h, t).wait_send()

    swap.wait_send()
    for share in shared:
        share.wait_send()
    delta_o[...] = outputs(1, recon_u) - clean_out

    for t in range(7):
        f3(1, t).wait_send()


def on_device(
    hidden_in, resid, down_one, gain_one, enc_weight, enc_bias, dec_weight, dec_bias, gain_pre, gate_two, up_two,
    down_two, gain_post,
):
    tiles = (T, 128)
    args = (
        hidden_in, resid, down_one, gain_one.reshape(tiles), enc_weight, enc_bias.reshape(1, 256), dec_weight,
        dec_bias.reshape(tiles), gain_pre.reshape(tiles), gate_two.T, up_two.T, down_two,
        gain_post.reshape(tiles),
    )
    held = {4: (D, 512), 5: (1, 512), 6: (512, D)}
    dma = pltpu.SemaphoreType.DMA
    vmem = pltpu.VMEM
    latents, delta = pl.pallas_call(
        kernel,
        name="spliced",
        out_shape=(vmem((128, 256), BF16), vmem((32, 128), F32)),
        in_specs=[pl.BlockSpec(memory_space=pl.ANY)] * len(args),
        out_specs=[pl.BlockSpec(memory_space=pltpu.VMEM)] * 2,
        scratch_shapes=[vmem(held.get(i, a.shape), a.dtype) for i, a in enumerate(args)]
        + [
            vmem((8, 112, 128), F32),
            vmem((8, 112, 128), BF16),
            vmem((8, 112, 128), BF16),
            vmem((112, 128), BF16),
            vmem((8, 112, 128), BF16),
            vmem((8, 112, 128), F32),
            vmem((112, 128), F32),
            vmem((112, 128), F32),
            vmem((4, 8, 896), F32),
            vmem((8, D), F32),
            vmem((8, D + 128), F32),
            vmem((16, 112, 128), BF16),
            vmem((2, 32, D), F32),
            vmem((64, D), BF16),
            vmem((64, 512), BF16),
            vmem((64, 256), BF16),
            vmem((64, 256), BF16),
            vmem((4, 64, 896), BF16),
            vmem((64, 896), F32),
            vmem((16, 16, 896), BF16),
            vmem((16, 896), BF16),
            vmem((8, 16, 896), BF16),
            vmem((8, 16, 896), BF16),
            vmem((32, D + 128), F32),
            vmem((32, D + 128), F32),
            vmem((2, 32, D), BF16),
            vmem((2, 8, 16, 896), BF16),
            vmem((2, 8, 16, 896), F32),
            vmem((2, 8, 16, 896), BF16),
            vmem((2, 16, 896), F32),
            vmem((2, 16, 896), BF16),
            vmem((2, 8, 16, 896), BF16),
            vmem((2, 32, 640), F32),
            vmem((2, 8, 128), F32),
            vmem((2, 8, 8, 128), F32),
            dma((7,)), dma((12,)),
            dma((3, 7)), dma((3, 7)), dma((3, 7)), dma((3, 7)),
            dma((3,)), dma((3,)), dma((15,)), dma((15,)), dma((1,)), dma((1,)),
            dma((3, 15)), dma((3, 15)), dma((3, 7)), dma((3, 7)), dma((3, 7)), dma((3, 7)),
            dma((2, 3, 7)), dma((2, 3, 7)), dma((2, 3, 7)), dma((2, 3, 7)), dma((2, 7)), dma((2, 7)),
        ],
        compiler_params=pltpu.CompilerParams(
            collective_id=0, has_side_effects=True, vmem_limit_bytes=62 * 2**20
        ),
        cost_estimate=pl.CostEstimate(flops=10**9, bytes_accessed=12 * 10**6, transcendentals=10**5),
    )(*args)
    return latents, delta[:, :56]


def solution(mesh):
    in_specs = (
        P("rows", "shard"),
        P("rows", None),
        P("shard", None),
        P(),
        P(None, ("rows", "shard")),
        P(("rows", "shard")),
        P(("rows", "shard"), None),
        P(),
        P(),
        P(None, "shard"),
        P(None, "shard"),
        P("shard", None),
        P(),
    )
    out_specs = (P(None, ("rows", "shard")), P("rows", "shard"))
    return jax.shard_map(on_device, mesh=mesh, in_specs=in_specs, out_specs=out_specs, check_vma=False)
```

```python
import functools

import jax
import jax.numpy as jnp
from jax import lax
from jax.experimental import pallas as pl
from jax.experimental.pallas import tpu as pltpu
from jax.sharding import PartitionSpec as P

D = 3584
T = D // 128
MESH = pl.DeviceIdType.MESH
F32, BF16 = jnp.float32, jnp.bfloat16
EPS = 1e-06


def pick(ref, start, rows):
    tile, turn = start // 128, lax.rem(start, 128)
    lo = ref[0:rows, pl.ds(pl.multiple_of(tile * 128, 128), 128)]
    hi = ref[0:rows, pl.ds(pl.multiple_of(tile * 128 + 128, 128), 128)]
    shift = lax.rem(128 - turn, 128)
    lane = lax.broadcasted_iota(jnp.int32, (rows, 128), 1)
    return jnp.where(lane < 128 - turn, pltpu.roll(lo, shift, 1), pltpu.roll(hi, shift, 1))


def around(t, n):
    return (n // 2 + n + (1 - 2 * (t % 2)) * ((t + 1) // 2)) % n


def gelu(v):
    return 0.5 * v * (1.0 + jnp.tanh(0.7978845608028654 * (v + 0.044715 * (v * v * v))))


def kernel(
    hid_h, resid_h, d1_h, g1_h, enc_h, eb_h, dec_h, db_h, gpre_h, gate_h, up_h, d2_h, gpost_h,
    lat_o, delta_o,
    hid, resid, d1, g1, enc, eb, dec, db, gpre, gate, up, d2, gpost,
    parts, parts_b, land_b1, send_b2, land_b2, resid_c, g1_c, db_c, db_row, gpre_row, gpost_row,
    clean_all, cent, lhs, lat, lat_src, lat_land, e_src, e_own, land_e1, send_e2, land_e2, recon_p,
    clean_u, recon_u, lhs_f, f_src, f_own, land_f1, f_sum, send_f2, land_f2, second, send_f3, land_f3,
    d1_sem, load_sem, s_b1, r_b1, s_b2, r_b2, s_w, r_w, s_c, r_c, s_l, r_l, s_e1, r_e1, s_e2, r_e2, s_e3, r_e3,
    s_f1, r_f1, s_f2, r_f2, s_f3, r_f3,
):
    r = lax.axis_index("rows")
    s = lax.axis_index("shard")
    yl, c = r // 2, lax.rem(r, 2)
    k, z = s // 8, lax.rem(s, 8)
    x, yh = k // 2, lax.rem(k, 2)
    y, m = 2 * yh + yl, yl * 8 + k
    other = (yl * 2 + 1 - c, s)

    def k_at(t):
        return lax.rem(x + around(t // 2, 4), 4) * 2 + lax.rem(yh + 1 - t % 2, 2)

    def k_from(t):
        return lax.rem(x + 4 - around(t // 2, 4), 4) * 2 + lax.rem(yh + 1 - t % 2, 2)

    def in_k(t):
        return (r, k_at(t) * 8 + z)

    def in_z(t):
        return (r, k * 8 + lax.rem(z + around(t, 8), 8))

    def plane_at(to_x, to_y):
        return (lax.rem(to_y, 2) * 2 + c, (to_x * 2 + to_y // 2) * 8 + z)

    def in_plane(t):
        return plane_at(lax.rem(x + around(t // 4, 4), 4), lax.rem(y + around(t % 4, 4), 4))

    def chunk_from(t):
        from_x = lax.rem(x + 4 - around(t // 4, 4), 4)
        from_y = lax.rem(y + 4 - around(t % 4, 4), 4)
        return lax.rem(from_y, 2) * 8 + from_x * 2 + from_y // 2

    def send(src, dst, s_sem, r_sem, device):
        return pltpu.make_async_remote_copy(
            src_ref=src, dst_ref=dst, send_sem=s_sem, recv_sem=r_sem, device_id=device, device_id_type=MESH
        )

    def first_load(g):
        cols = pl.ds(512 * g, 512)
        return pltpu.make_async_copy(d1_h.at[:, cols], d1.at[:, cols], d1_sem.at[g])

    loads = [
        pltpu.make_async_copy(a, b, load_sem.at[i])
        for i, (a, b) in enumerate(
            (
                (hid_h, hid), (resid_h, resid), (g1_h, g1), (db_h, db), (gpre_h, gpre), (gpost_h, gpost),
                (eb_h, eb.at[:, pl.ds(0, 256)]), (enc_h, enc.at[:, pl.ds(0, 256)]), (dec_h, dec.at[pl.ds(0, 256), :]),
                (gate_h, gate), (up_h, up), (d2_h, d2),
            )
        )
    ]
    loads[0].start()
    for g in range(7):
        first_load(g).start()

    barrier = pltpu.get_barrier_semaphore()
    for t in range(15):
        pl.semaphore_signal(barrier, inc=1, device_id=in_plane(t), device_id_type=MESH)
    for t in range(7):
        pl.semaphore_signal(barrier, inc=1, device_id=in_z(t), device_id_type=MESH)

    pl.semaphore_signal(barrier, inc=1, device_id=other, device_id_type=MESH)

    thirds = ((0, 32), (32, 32), (64, 48))

    def b1(h, t):
        rows = pl.ds(*thirds[h])
        return send(
            parts_b.at[k_at(t), rows, :], land_b1.at[t, rows, :], s_b1.at[h, t], r_b1.at[h, t], in_k(t)
        )

    loads[0].wait()
    for g in range(7):
        first_load(g).wait()
        part = jnp.dot(hid[...], d1[:, 512 * g : 512 * g + 512], preferred_element_type=F32)
        for j in range(4):
            row = 4 * (4 * g + j)
            for piece in range(8):
                parts[piece, row : row + 4, :] = part[4 * piece : 4 * piece + 4, 128 * j : 128 * j + 128]
        if g in (1, 3, 6):
            h = (1, 3, 6).index(g)
            rows = slice(thirds[h][0], sum(thirds[h]))
            for piece in range(8):
                parts_b[piece, rows, :] = parts[piece, rows, :].astype(BF16)
            if h == 0:
                pl.semaphore_wait(barrier, 23)
            for t in range(7):
                b1(h, t).start()

    for load in loads[1:]:
        load.start()
    shared = [
        send(a, b, s_w.at[i], r_w.at[i], other)
        for i, (a, b) in enumerate(
            (
                (eb_h, eb.at[:, pl.ds(256, 256)]),
                (enc_h, enc.at[:, pl.ds(256, 256)]),
                (dec_h, dec.at[pl.ds(256, 256), :]),
            )
        )
    ]
    for share in shared:
        share.start()

    for i in range(1, 7):
        loads[i].wait()
    for j in range(T):
        tile = slice(128 * j, 128 * j + 128)
        old = resid[:, tile].astype(F32)
        for piece in range(8):
            resid_c[piece, 4 * j : 4 * j + 4, :] = old[4 * piece : 4 * piece + 4, :]
        g1_c[4 * j : 4 * j + 4, :] = jnp.broadcast_to(g1[j : j + 1, :], (4, 128))
        db_c[4 * j : 4 * j + 4, :] = jnp.broadcast_to(db[j : j + 1, :], (4, 128))
        gpre_row[:, tile] = jnp.broadcast_to(gpre[j : j + 1, :], (8, 128))
        gpost_row[:, tile] = jnp.broadcast_to(gpost[j : j + 1, :], (8, 128))
        db_row[j // 7, :, 128 * (j % 7) : 128 * (j % 7) + 128] = jnp.broadcast_to(db[j : j + 1, :], (8, 128))
    gpost_row[:, D:] = jnp.zeros((8, 128), F32)
    clean_u[:, D:] = jnp.zeros((32, 128), F32)
    recon_u[:, D:] = jnp.zeros((32, 128), F32)
    second[:, :, 448:] = jnp.zeros((2, 32, 192), F32)

    def b2(h, t):
        rows = pl.ds(*thirds[h])
        return send(send_b2.at[rows, :], land_b2.at[t, rows, :], s_b2.at[h, t], r_b2.at[h, t], in_z(t))

    sums = []
    for h, (low, count) in enumerate(thirds):
        for t in range(7):
            b1(h, t).wait_recv()
        total = parts[k, low : low + count, :]
        for t in range(7):
            total += land_b1[t, low : low + count, :].astype(F32)
        send_b2[low : low + count, :] = total.astype(BF16)
        for t in range(7):
            b2(h, t).start()

        sums.append(total)

    for h, (low, count) in enumerate(thirds):
        for t in range(7):
            b2(h, t).wait_recv()
        for t in range(7):
            sums[h] += land_b2[t, low : low + count, :].astype(F32)
    total = jnp.concatenate(sums, axis=0)
    squares = total[0:8] * total[0:8]
    for i in range(1, 14):
        squares += total[8 * i : 8 * i + 8] * total[8 * i : 8 * i + 8]
    squares += pltpu.roll(squares, 4, 0)
    scale = lax.rsqrt(jnp.sum(squares, axis=1, keepdims=True) / D + EPS)
    scale = jnp.concatenate([jnp.broadcast_to(scale, (8, 128))] * 14, axis=0)
    clean_all[m] = (resid_c[k] + total * scale * g1_c[...]).astype(BF16)

    def spread(t):
        return send(clean_all.at[m], clean_all.at[m], s_c.at[t], r_c.at[t], in_plane(t))

    for t in range(15):
        spread(t).start()

    for t in range(15):
        at = chunk_from(t)
        send(clean_all.at[at], clean_all.at[at], s_c.at[t], r_c.at[t], in_plane(t)).wait_recv()

    for low in range(2):
        for q in range(8):
            centered = (clean_all[low * 8 + q].astype(F32) - db_c[...]).astype(BF16).astype(F32)
            for j in range(T):
                cent[low, 4 * q : 4 * q + 4, 128 * j : 128 * j + 128] = centered[4 * j : 4 * j + 4, :]
        lhs[32 * low : 32 * low + 32, :] = cent[low].astype(BF16)

    loads[7].wait()
    for share in shared:
        share.wait_recv()
    pre_act = jnp.dot(lhs[...], enc[...], preferred_element_type=F32) + eb[...]
    lat[...] = jnp.maximum(pre_act, 0.0).astype(BF16)
    lat_src[...] = lat[:, 256:512]
    swap = send(lat_src, lat_land, s_l.at[0], r_l.at[0], other)

    cuts = ((0, 384), (384, 256), (640, 256))

    def e1(h, t):
        to_x, to_y = lax.rem(x + around(t // 4, 4), 4), lax.rem(y + around(t % 4, 4), 4)
        rows = pl.ds(pl.multiple_of(32 * lax.rem(to_y, 2) + 16 * (to_y // 2), 16), 16)
        cols = pl.ds(*cuts[h])
        return send(
            e_src.at[t // 4, rows, cols], land_e1.at[t, :, cols], s_e1.at[h, t], r_e1.at[h, t], plane_at(to_x, to_y)
        )

    loads[8].wait()
    for h, (low, count) in enumerate(cuts):
        for g in range(4):
            first_col = lax.rem(x + around(g, 4), 4) * 896 + low
            cols = pl.ds(pl.multiple_of(first_col, 128), count)
            own = jnp.dot(lat[...], dec[:, cols], preferred_element_type=F32)
            if g == 3:
                e_own[:, low : low + count] = own
            e_src[g, :, low : low + count] = own.astype(BF16)
            for t in range(4 * g, min(4 * g + 4, 15)):
                e1(h, t).start()

    swap.start()

    def layer(h, stream):
        squares = jnp.zeros((32, 128), F32)
        for j in range(T):
            tile = stream[:, 128 * j : 128 * j + 128]
            squares += tile * tile
        scale = lax.rsqrt(jnp.sum(squares, axis=1, keepdims=True) / D + EPS)
        for g in range(7):
            cols = slice(512 * g, 512 * g + 512)
            lhs_f[h, :, cols] = (stream[:, cols] * scale * gpre_row[0:1, cols]).astype(BF16)
        gate_out = lax.dot_general(lhs_f[h], gate[...], (((1,), (1,)), ((), ())), preferred_element_type=F32)
        up_out = lax.dot_general(lhs_f[h], up[...], (((1,), (1,)), ((), ())), preferred_element_type=F32)
        act = (gelu(gate_out) * up_out).astype(BF16)
        for g in range(4):
            part = jnp.dot(act, d2[:, 896 * g : 896 * g + 896], preferred_element_type=F32)
            for half in range(2):
                piece = part[:, 448 * half : 448 * half + 448]
                top, low = piece[0:16, :], piece[16:32, :]
                ends = jnp.concatenate([top[:, 384:448], low[:, 384:448]], axis=1)
                packed = jnp.concatenate([top[:, 0:384], low[:, 0:384], ends], axis=1)
                f_own[h, 2 * g + half] = packed
                f_src[h, 2 * g + half] = packed.astype(BF16)

    for q in range(8):
        clean = clean_all[yl * 8 + q].astype(F32)
        for j in range(T):
            clean_u[4 * q : 4 * q + 4, 128 * j : 128 * j + 128] = clean[4 * j : 4 * j + 4, :]
    loads[9].wait()
    loads[10].wait()
    loads[11].wait()
    layer(0, clean_u)

    row = pl.multiple_of(32 * yl + 16 * yh, 16)

    def e2(h, t):
        cols = pl.ds(*cuts[h])
        return send(send_e2.at[:, cols], land_e2.at[t, :, cols], s_e2.at[h, t], r_e2.at[h, t], in_z(t))

    def e3(h, t, at):
        cols = pl.ds(*cuts[h])
        return send(recon_p.at[at, :, cols], recon_p.at[at, :, cols], s_e3.at[h, t], r_e3.at[h, t], in_k(t))

    def f1(h, q, t):
        cols = pl.ds(*cuts[q])
        return send(
            f_src.at[h, k_at(t), :, cols], land_f1.at[h, t, :, cols], s_f1.at[h, q, t], r_f1.at[h, q, t], in_k(t)
        )

    def f2(h, q, t):
        cols = pl.ds(*cuts[q])
        return send(
            send_f2.at[h, :, cols], land_f2.at[h, t, :, cols], s_f2.at[h, q, t], r_f2.at[h, q, t], in_z(t)
        )

    def f3(h, t):
        return send(send_f3.at[h], land_f3.at[h, t], s_f3.at[h, t], r_f3.at[h, t], in_k(t))

    def start_f1(h):
        for q in range(3):
            for t in range(7):
                f1(h, q, t).start()

    sums = []
    for h, (low, count) in enumerate(cuts):
        for t in range(15):
            e1(h, t).wait_recv()
        total = e_own[pl.ds(row, 16), low : low + count]
        for t in range(15):
            total += land_e1[t, :, low : low + count].astype(F32)
        send_e2[:, low : low + count] = total.astype(BF16)
        for t in range(7):
            e2(h, t).start()

        sums.append(total)

    start_f1(0)

    for h, (low, count) in enumerate(cuts):
        for t in range(7):
            e2(h, t).wait_recv()
        for t in range(7):
            sums[h] += land_e2[t, :, low : low + count].astype(F32)
        recon_p[k, :, low : low + count] = (sums[h] + db_row[x, 0:1, low : low + count]).astype(BF16)
        for t in range(7):
            e3(h, t, k).start()

    def sum_over_k(h):
        for q, (low, count) in enumerate(cuts):
            cols = slice(low, low + count)
            for t in range(7):
                f1(h, q, t).wait_recv()
            total = f_own[h, k, :, cols]
            for t in range(7):
                total += land_f1[h, t, :, cols].astype(F32)
            f_sum[h, :, cols] = total
            send_f2[h, :, cols] = total.astype(BF16)
            for t in range(7):
                f2(h, q, t).start()

    diagonal = (
        lax.broadcasted_iota(jnp.int32, (32, 128), 0) == lax.broadcasted_iota(jnp.int32, (32, 128), 1)
    ).astype(F32)

    def sum_over_z(h):
        for q, (low, count) in enumerate(cuts):
            cols = slice(low, low + count)
            for t in range(7):
                f2(h, q, t).wait_recv()
            total = f_sum[h, :, cols]
            for t in range(7):
                total += land_f2[h, t, :, cols].astype(F32)
            f_sum[h, :, cols] = total
        second[h, 0:16, 0:384] = f_sum[h, :, 0:384]
        second[h, 16:32, 0:384] = f_sum[h, :, 384:768]
        second[h, 0:16, 384:448] = f_sum[h, :, 768:832]
        second[h, 16:32, 384:448] = f_sum[h, :, 832:896]
        total = second[h, :, 0:512]
        squares = jnp.sum(total * total, axis=1, keepdims=True)
        flat = jnp.sum(squares * diagonal, axis=0, keepdims=True)
        send_f3[h] = jnp.broadcast_to(flat, (8, 128))
        for t in range(7):
            f3(h, t).start()

    def outputs(h, stream):
        for t in range(7):
            f3(h, t).wait_recv()
        flat = send_f3[h]
        for t in range(7):
            flat += land_f3[h, t]
        squares = jnp.sum(flat[0:1, :] * diagonal, axis=1, keepdims=True)
        gain = pick(gpost_row, 56 * s, 8)[0:1, :]
        return pick(stream, 56 * s, 32) + pick(second.at[h], 56 * z, 32) * lax.rsqrt(squares / D + EPS) * gain


    for h in range(3):
        for t in range(7):
            e3(h, t, k_from(t)).wait_recv()
    for q in range(8):
        row, col = 16 * (q % 2), 896 * (q // 2)
        recon_u[row : row + 16, col : col + 896] = recon_p[q].astype(F32)
    layer(1, recon_u)

    start_f1(1)
    sum_over_k(0)

    sum_over_k(1)
    sum_over_z(0)
    sum_over_z(1)
    clean_out = outputs(0, clean_u)
    swap.wait_recv()
    for low in range(2):
        rows = slice(32 * low, 32 * low + 32)
        lat_o[pl.ds(pl.multiple_of(64 * low + 32 * c, 32), 32), :] = lat[rows, 0:256]
        lat_o[pl.ds(pl.multiple_of(64 * low + 32 - 32 * c, 32), 32), :] = lat_land[rows, :]

    for t in range(7):
        for h in range(3):
            b1(h, t).wait_send()
            b2(h, t).wait_send()
            e2(h, t).wait_send()
            e3(h, t, k).wait_send()
        f3(0, t).wait_send()
        for h in range(2):
            for q in range(3):
                f1(h, q, t).wait_send()
                f2(h, q, t).wait_send()
    for t in range(15):
        spread(t).wait_send()
        for h in range(3):
            e1(h, t).wait_send()

    swap.wait_send()
    for share in shared:
        share.wait_send()
    delta_o[...] = outputs(1, recon_u) - clean_out

    for t in range(7):
        f3(1, t).wait_send()


def on_device(
    hidden_in, resid, down_one, gain_one, enc_weight, enc_bias, dec_weight, dec_bias, gain_pre, gate_two, up_two,
    down_two, gain_post,
):
    tiles = (T, 128)
    args = (
        hidden_in, resid, down_one, gain_one.reshape(tiles), enc_weight, enc_bias.reshape(1, 256), dec_weight,
        dec_bias.reshape(tiles), gain_pre.reshape(tiles), gate_two.T, up_two.T, down_two,
        gain_post.reshape(tiles),
    )
    held = {4: (D, 512), 5: (1, 512), 6: (512, D)}
    dma = pltpu.SemaphoreType.DMA
    vmem = pltpu.VMEM
    latents, delta = pl.pallas_call(
        kernel,
        name="spliced",
        out_shape=(vmem((128, 256), BF16), vmem((32, 128), F32)),
        in_specs=[pl.BlockSpec(memory_space=pl.ANY)] * len(args),
        out_specs=[pl.BlockSpec(memory_space=pltpu.VMEM)] * 2,
        scratch_shapes=[vmem(held.get(i, a.shape), a.dtype) for i, a in enumerate(args)]
        + [
            vmem((8, 112, 128), F32),
            vmem((8, 112, 128), BF16),
            vmem((8, 112, 128), BF16),
            vmem((112, 128), BF16),
            vmem((8, 112, 128), BF16),
            vmem((8, 112, 128), F32),
            vmem((112, 128), F32),
            vmem((112, 128), F32),
            vmem((4, 8, 896), F32),
            vmem((8, D), F32),
            vmem((8, D + 128), F32),
            vmem((16, 112, 128), BF16),
            vmem((2, 32, D), F32),
            vmem((64, D), BF16),
            vmem((64, 512), BF16),
            vmem((64, 256), BF16),
            vmem((64, 256), BF16),
            vmem((4, 64, 896), BF16),
            vmem((64, 896), F32),
            vmem((16, 16, 896), BF16),
            vmem((16, 896), BF16),
            vmem((8, 16, 896), BF16),
            vmem((8, 16, 896), BF16),
            vmem((32, D + 128), F32),
            vmem((32, D + 128), F32),
            vmem((2, 32, D), BF16),
            vmem((2, 8, 16, 896), BF16),
            vmem((2, 8, 16, 896), F32),
            vmem((2, 8, 16, 896), BF16),
            vmem((2, 16, 896), F32),
            vmem((2, 16, 896), BF16),
            vmem((2, 8, 16, 896), BF16),
            vmem((2, 32, 640), F32),
            vmem((2, 8, 128), F32),
            vmem((2, 8, 8, 128), F32),
            dma((7,)), dma((12,)),
            dma((3, 7)), dma((3, 7)), dma((3, 7)), dma((3, 7)),
            dma((3,)), dma((3,)), dma((15,)), dma((15,)), dma((1,)), dma((1,)),
            dma((3, 15)), dma((3, 15)), dma((3, 7)), dma((3, 7)), dma((3, 7)), dma((3, 7)),
            dma((2, 3, 7)), dma((2, 3, 7)), dma((2, 3, 7)), dma((2, 3, 7)), dma((2, 7)), dma((2, 7)),
        ],
        compiler_params=pltpu.CompilerParams(
            collective_id=0, has_side_effects=True, vmem_limit_bytes=62 * 2**20
        ),
        cost_estimate=pl.CostEstimate(flops=10**9, bytes_accessed=12 * 10**6, transcendentals=10**5),
    )(*args)
    return latents, delta[:, :56]


def solution(mesh):
    in_specs = (
        P("rows", "shard"),
        P("rows", None),
        P("shard", None),
        P(),
        P(None, ("rows", "shard")),
        P(("rows", "shard")),
        P(("rows", "shard"), None),
        P(),
        P(),
        P(None, "shard"),
        P(None, "shard"),
        P("shard", None),
        P(),
    )
    out_specs = (P(None, ("rows", "shard")), P("rows", "shard"))
    return jax.shard_map(on_device, mesh=mesh, in_specs=in_specs, out_specs=out_specs, check_vma=False)
```
